256 devices in a mesh: grp: 8 (over z), seq: 32 (over y, x, core).
Axes of the slice: x: 4, y: 4, z: 8, core: 2. Of those that a mesh axis runs over, the one named last changes fastest.
Arguments:
- loader_layer_input: bfloat16 [32768, 8192], P('seq', 'grp'), may hold values from -6 to 6
- loader_output_gradient: bfloat16 [32768, 2048], P('seq', 'grp'), may hold values from -0.049804688 to 0.049804688
- trial_per_block: int32 [1024, 1], P('seq'), may hold values from 0 to 31; in each aligned block of 32 rows (0 to 31, 32 to 63, ...) at most 2 rows name the same one
- trial_slot_index: int32 [32], replicated, may hold values from 0 to 31, each once
- frozen_weight: bfloat16 [8192, 2048], P('grp'), may hold values from -0.0625 to 0.0625
- down_adapters: bfloat16 [32, 8192, 64], P(None, 'grp'), may hold values from -0.0625 to 0.0625
- up_adapters: bfloat16 [32, 64, 2048], P(None, None, 'grp'), may hold values from -0.75 to 0.75
Outputs:
- output: bfloat16 [32768, 2048], P('seq', 'grp')
- down_adapter_gradient: float32 [32, 8192, 64], P('seq', 'grp')
- up_adapter_gradient: float32 [32, 64, 2048], P('seq', None, 'grp')
The draws below stay inside these ranges and needn't reach their ends.
Inputs may be any that keep to these rules, and one draw needn't show every extreme that they name: `trial_per_block`: in every aligned group of 32 rows (one data shard's blocks) no trial appears more than 2 times. `trial_slot_index`: A permutation of the trials; slot k is held by index k // 1 of seq.
All inputs are finite; a program needn't handle non-finite values.
Results may differ from the reference program's by a relative error of at most 0.0046.
Values may be sent and summed in bfloat16 or wider, within the bound.
A program may use at most 128 MiB of HBM per device.

```python
import math
import jax
import jax.numpy as jnp
import numpy as np
from jax import lax

MODEL_WIDTH = 8192
KEY_VALUE_WIDTH = 2048
ADAPTER_RANK = 64
TRIAL_COUNT = 32
MOST = 2
BLK = 32
TOKENS = 32768
NBLOCKS = 1024
N_SEQ = 32


def block_levels(own_key, extent, split, least, top_value):
    loudness = 1.0
    for axis_at, shards_of in split:
        steps = jax.random.uniform(jax.random.fold_in(jax.random.fold_in(own_key, 6), axis_at), (shards_of,), jnp.float32, least / len(split), top_value / len(split))
        loudness = loudness * jnp.repeat(jnp.exp(steps), extent[axis_at] // shards_of).reshape((-1,) + (1,) * (len(extent) - 1 - axis_at))
    return loudness


def routed_block(own_key, own, number, rows, number_of, top, limit, slope):
    ranking = jax.random.permutation(own_key, number_of)
    packed, common = load_shares(number_of, rows * top, limit, slope, True), load_shares(number_of, rows * top, limit, slope, False)
    places = jnp.arange(number_of)

    def named(tallies, turn):
        used = int((tallies > 0).sum())
        fixed = max(1, used // 4)
        moved = fixed + (places - fixed + turn * (used - fixed)) % max(1, number_of - fixed)
        return jnp.zeros((number_of,), jnp.int32).at[ranking[jnp.where(places < fixed, places, moved)]].set(jnp.asarray(tallies, jnp.int32))

    tallies = jnp.where(number % 4 == 0, named(packed, number // 4), named(common, number - number // 4 - 1))
    mixed = jax.random.permutation(jax.random.fold_in(own, 3), number_of)
    giver, sink = mixed[0:number_of // 2 * 2:2], mixed[1:number_of // 2 * 2:2]
    room = jnp.minimum(tallies[giver] - 1, limit - tallies[sink]) // 2
    room = jnp.where((giver == ranking[0]) | (sink == ranking[0]) | (tallies[sink] == 0), 0, jnp.maximum(room, 0))
    moved = jax.random.randint(jax.random.fold_in(own, 4), (number_of // 2,), 0, 1 << 20) % (room + 1)
    tallies = tallies.at[giver].add(-moved).at[sink].add(moved)
    labels = jnp.searchsorted(jnp.cumsum(tallies), jnp.arange(rows * top), side="right").astype(jnp.int32)
    listing = labels.reshape(top, rows).T
    listing = listing[jax.random.permutation(jax.random.fold_in(own, 1), rows)]
    turn = jax.random.randint(jax.random.fold_in(own, 2), (rows, 1), 0, top)
    return jnp.take_along_axis(listing, (jnp.arange(top)[None, :] + turn) % top, axis=1)


def load_shares(number_of, total, limit, lean, full):
    loads = [(1 << 20) // math.isqrt(grade ** lean) + 1 for grade in range(1, number_of + 1)]
    largest = limit if full else min(limit, max(-(-total // number_of), total * loads[0] // sum(loads)))
    least = 1 if total - largest >= number_of - 1 else 0
    holding, spare = [largest] + [least] * (number_of - 1), total - largest - least * (number_of - 1)
    while spare > 0:
        candidates = [i for i in range(1, number_of) if holding[i] < largest] or [i for i in range(1, number_of) if holding[i] < limit]
        pool, remaining = sum([loads[i] for i in candidates]), spare
        for i in candidates:
            extra = min(limit - holding[i], max(1, remaining * loads[i] // pool), spare)
            holding[i] = holding[i] + extra
            spare = spare - extra
    return np.array(holding)


def noise(stream_key, dims, width, limit, cuts=(), kind=jnp.bfloat16):
    values = jax.random.normal(stream_key, dims, jnp.float32) * width
    if len(cuts) > 0:
        values = block_levels(stream_key, dims, cuts, -0.22, 0.18) * values
    return jnp.clip(values, min=-limit, max=limit).astype(kind)


def setup_inputs(seed: int = 0) -> dict:
    key_list = jax.random.split(jax.random.key(seed), 8)
    loader_layer_input = noise(key_list[0], (TOKENS, MODEL_WIDTH), 1.0, 6.0, ((0, 32), (1, 8)))
    loader_output_gradient = noise(key_list[1], (TOKENS, KEY_VALUE_WIDTH), 0.008, 0.049804688, ((0, 32), (1, 8)))
    trial_per_block_keys = jax.random.split(jax.random.fold_in(key_list[2], 1), NBLOCKS // N_SEQ)
    trial_per_block_turns = jax.random.permutation(jax.random.fold_in(key_list[2], 3), NBLOCKS // N_SEQ)
    trial_per_block = jax.vmap(lambda own, number: routed_block(jax.random.fold_in(key_list[2], 2), own, number, N_SEQ, TRIAL_COUNT, 1, MOST, 2))(trial_per_block_keys, trial_per_block_turns).reshape((NBLOCKS, 1))
    trial_slot_index = jax.random.permutation(key_list[3], TRIAL_COUNT).astype(jnp.int32)
    frozen_weight = noise(key_list[4], (MODEL_WIDTH, KEY_VALUE_WIDTH), MODEL_WIDTH ** -0.5, 0.0625, ((0, 8),))
    down_adapters = noise(key_list[5], (TRIAL_COUNT, MODEL_WIDTH, ADAPTER_RANK), MODEL_WIDTH ** -0.5, 0.0625, ((1, 8),))
    up_adapters = noise(key_list[6], (TRIAL_COUNT, ADAPTER_RANK, KEY_VALUE_WIDTH), ADAPTER_RANK ** -0.5, 0.75, ((2, 8),))
    return dict(loader_layer_input=loader_layer_input, loader_output_gradient=loader_output_gradient, trial_per_block=trial_per_block, trial_slot_index=trial_slot_index, frozen_weight=frozen_weight, down_adapters=down_adapters, up_adapters=up_adapters)


ADAPTER_SCALE = 2.0


def reference(loader_layer_input, loader_output_gradient, trial_per_block, trial_slot_index, frozen_weight, down_adapters, up_adapters):
    token_count = loader_layer_input.shape[0]
    frozen_output = jnp.dot(loader_layer_input, frozen_weight, preferred_element_type=jnp.float32)
    blocks = trial_per_block.shape[0]
    input_block_list = loader_layer_input.reshape(blocks, BLK, MODEL_WIDTH)
    gradient_block_list = loader_output_gradient.reshape(blocks, BLK, KEY_VALUE_WIDTH)

    def step(carry, item):
        accumulator_down, accumulator_up = carry
        input_block, gradient_block, trial_number = item
        down_weight = down_adapters[trial_number]
        up_weight = up_adapters[trial_number]
        adapter_down_projection = jnp.dot(input_block, down_weight, preferred_element_type=jnp.float32).astype(jnp.bfloat16)
        adapter_backward = jnp.dot(gradient_block, up_weight.T, preferred_element_type=jnp.float32).astype(jnp.bfloat16)
        adapter_branch = jnp.dot(adapter_down_projection, up_weight, preferred_element_type=jnp.float32)
        accumulator_down = accumulator_down.at[trial_number].add(jnp.dot(input_block.T, adapter_backward, preferred_element_type=jnp.float32))
        accumulator_up = accumulator_up.at[trial_number].add(jnp.dot(adapter_down_projection.T, gradient_block, preferred_element_type=jnp.float32))
        return (accumulator_down, accumulator_up), adapter_branch

    start = (jnp.zeros((TRIAL_COUNT, MODEL_WIDTH, ADAPTER_RANK), jnp.float32), jnp.zeros((TRIAL_COUNT, ADAPTER_RANK, KEY_VALUE_WIDTH), jnp.float32))
    (accumulator_down, accumulator_up), adapter_branches = lax.scan(step, start, (input_block_list, gradient_block_list, trial_per_block[:, 0].astype(jnp.int32)))
    combined_output = (frozen_output + ADAPTER_SCALE * adapter_branches.reshape(token_count, KEY_VALUE_WIDTH)).astype(jnp.bfloat16)
    output = combined_output.reshape(N_SEQ, N_SEQ, BLK, KEY_VALUE_WIDTH).transpose(1, 0, 2, 3).reshape(token_count, KEY_VALUE_WIDTH)
    down_adapter_gradient = jnp.zeros((TRIAL_COUNT, MODEL_WIDTH, ADAPTER_RANK), jnp.float32).at[trial_slot_index].set(ADAPTER_SCALE * accumulator_down)
    up_adapter_gradient = jnp.zeros((TRIAL_COUNT, ADAPTER_RANK, KEY_VALUE_WIDTH), jnp.float32).at[trial_slot_index].set(ADAPTER_SCALE * accumulator_up)
    return (output, down_adapter_gradient, up_adapter_gradient)
```

```python
import jax
import jax.numpy as jnp
from jax import lax
from jax.sharding import PartitionSpec as P

ADAPTER_SCALE = 2.0


def local(x, g, trial_per_block, trial_slot_index, w, down, up):
    blocks = trial_per_block.shape[0]
    trials, depth, rank = down.shape
    cols = up.shape[2]
    blk = x.shape[0] // blocks
    trial = trial_per_block[:, 0]
    one_hot = (trial[:, None] == jnp.arange(trials, dtype=jnp.int32)[None, :]).astype(jnp.bfloat16)
    slot_hot = (trial_slot_index[:, None] == jnp.arange(trials, dtype=jnp.int32)[None, :]).astype(jnp.bfloat16)
    block_slot = jnp.dot(one_hot, slot_hot)
    xb = x.reshape(blocks, blk, depth)
    gb = g.reshape(blocks, blk, cols)
    down_b = jnp.einsum("bt,tfr->bfr", one_hot, down)
    up_b = jnp.einsum("bt,tro->bro", one_hot, up)
    down_part = jnp.einsum("bpf,bfr->bpr", xb, down_b, preferred_element_type=jnp.float32)
    back_part = jnp.einsum("bpo,bro->bpr", gb, up_b, preferred_element_type=jnp.float32)
    down_total, back_total = lax.psum((down_part, back_part), "grp")
    ld = down_total.astype(jnp.bfloat16)
    lb = back_total.astype(jnp.bfloat16)
    part = jnp.dot(x, w, preferred_element_type=jnp.float32)
    frozen = lax.psum_scatter(part, "grp", scatter_dimension=1, tiled=True)
    lb_all = (lb[:, :, None, :] * block_slot[:, None, :, None]).reshape(blocks * blk, trials * rank)
    ld_all = (ld[:, :, None, :] * block_slot[:, None, :, None]).reshape(blocks * blk, trials * rank)
    down_dense = jnp.einsum("nf,nq->qf", x, lb_all, preferred_element_type=jnp.float32)
    up_dense = jnp.einsum("nq,no->qo", ld_all, g, preferred_element_type=jnp.float32)
    both = jnp.concatenate([down_dense.reshape(trials, rank, depth), up_dense.reshape(trials, rank, cols)], axis=2)
    total = ADAPTER_SCALE * lax.psum_scatter(both, "seq", scatter_dimension=0, tiled=True)
    branch = jnp.einsum("bpr,bro->bpo", ld, up_b, preferred_element_type=jnp.float32)
    mixed = (frozen + ADAPTER_SCALE * branch.reshape(frozen.shape)).astype(jnp.bfloat16)
    out = lax.all_to_all(mixed, "seq", split_axis=0, concat_axis=0, tiled=True)
    return out, jnp.transpose(total[:, :, :depth], (0, 2, 1)), total[:, :, depth:]


def solution(mesh):
    in_specs = (
        P("seq", "grp"),
        P("seq", "grp"),
        P("seq", None),
        P(),
        P("grp", None),
        P(None, "grp", None),
        P(None, None, "grp"),
    )
    out_specs = (P("seq", "grp"), P("seq", "grp", None), P("seq", None, "grp"))
    return jax.shard_map(local, mesh=mesh, in_specs=in_specs, out_specs=out_specs, check_vma=False)
```

```python
import jax
import jax.numpy as jnp
from jax import lax
from jax.experimental import pallas as pl
from jax.experimental.pallas import tpu as pltpu
from jax.sharding import PartitionSpec as P

ADAPTER_SCALE = 2.0
MESH = pl.DeviceIdType.MESH
F32, BF16 = jnp.float32, jnp.bfloat16
NT = (((1,), (1,)), ((), ()))
TN = (((0,), (0,)), ((), ()))
Z, Y, X, C = 8, 4, 4, 2
SEQ = Y * X * C
CHUNKS = 4


def loop(n, body):
    lax.fori_loop(0, n, lambda i, c: (body(i), c)[1], 0)


def kernel(
    meta, x_h, g_h, w_h, d_h, u_h, out_h, ga_o, gb_o,
    xv, gv, wv, dv, uv, sbuf, rbuf, lp, lsb, lrb, lall, s1, r1, sg, ra, rb, ta, tb, ra3, rb3, fin, branch, mix,
    ld_sem, zs, zr, ls, lr, ags, agr, s1s, s1r, ras, rar, rbs, rbr, tas, tar, tbs, tbr, os, orr, loc,
):
    zi, si = lax.axis_index("grp"), lax.axis_index("seq")
    ci, xi, yi = si % C, (si // C) % X, si // (C * X)
    blocks, blk, depth = xv.shape
    cols = gv.shape[2]
    rank = dv.shape[1]
    half = rank // 2
    per = blocks // CHUNKS
    wide = depth + cols

    def seq_at(y, x, c):
        return (y * X + x) * C + c

    barrier = pltpu.get_barrier_semaphore()
    loop(SEQ - 1, lambda o: pl.semaphore_signal(barrier, inc=1, device_id={"seq": (si + o + 1) % SEQ}, device_id_type=MESH))
    loop(Z - 1, lambda o: pl.semaphore_signal(barrier, inc=1, device_id={"grp": (zi + o + 1) % Z}, device_id_type=MESH))

    def w_copy(r):
        at = pl.multiple_of(((zi + r) % Z) * cols, cols)
        return pltpu.make_async_copy(w_h.at[:, pl.ds(at, cols)], wv.at[r], ld_sem.at[r])

    x_copy = pltpu.make_async_copy(x_h, xv, ld_sem.at[8])
    g_copy = pltpu.make_async_copy(g_h, gv, ld_sem.at[9])
    d_copy = pltpu.make_async_copy(d_h, dv, ld_sem.at[10])
    u_copy = pltpu.make_async_copy(u_h, uv, ld_sem.at[11])
    x_copy.start()
    w_copy(4).start()
    d_copy.start()
    g_copy.start()
    u_copy.start()
    for r in (3, 5, 2, 6, 1, 7, 0):
        w_copy(r).start()

    def rows_of(q):
        return ((yi + q + 1) % Y) * per

    def own(q, r):
        rows = xv[pl.ds(rows_of(q), per)].reshape(per * blk, depth)
        return jnp.dot(rows, wv[r], preferred_element_type=F32)

    def z_copy(dr, q, d):
        return pltpu.make_async_remote_copy(
            src_ref=sbuf.at[dr, q, d - 1], dst_ref=rbuf.at[dr, q, d - 1],
            send_sem=zs.at[dr, q, d - 1], recv_sem=zr.at[dr, q, d - 1],
            device_id={"grp": (zi + 1 - 2 * dr + Z) % Z}, device_id_type=MESH,
        )

    def event(dr, q, d, first):
        v = own(q, ((1 - 2 * dr) * d + Z) % Z)
        if not first:
            z_copy(dr, q, d + 1).wait_recv()
            v = v + rbuf[dr, q, d].astype(F32)
        sbuf[dr, q, d - 1] = v.astype(BF16)
        z_copy(dr, q, d).start()

    def l_copy(dr, h, d):
        return pltpu.make_async_remote_copy(
            src_ref=lsb.at[dr, h, d - 1], dst_ref=lrb.at[dr, h, d - 1],
            send_sem=ls.at[dr, h, d - 1], recv_sem=lr.at[dr, h, d - 1],
            device_id={"grp": (zi + 1 - 2 * dr + Z) % Z}, device_id_type=MESH,
        )

    def l_rows(r, h):
        return pl.ds(((zi + r) % Z) * 4 + 2 * h, 2)

    def l_step(d):
        for h in range(2):
            for dr in range(2):
                length = 4 if h == dr else 3
                if d > length:
                    continue
                v = lp[l_rows(((1 - 2 * dr) * d + Z) % Z, h)]
                if d < length:
                    l_copy(dr, h, d + 1).wait_recv()
                    v = v + lrb[dr, h, d]
                lsb[dr, h, d - 1] = v
                l_copy(dr, h, d).start()

    def gather_copy(o, source):
        at = pl.ds(source * 4, 4)
        return pltpu.make_async_remote_copy(
            src_ref=lall.at[at], dst_ref=lall.at[at], send_sem=ags.at[o - 1], recv_sem=agr.at[o - 1],
            device_id={"grp": (zi + o) % Z}, device_id_type=MESH,
        )

    x_copy.wait()
    w_copy(4).wait()
    pl.semaphore_wait(barrier, SEQ - 1 + Z - 1)

    loop(4, lambda i: event(i % 2, 2 * (i % 2) + i // 2, 4, True))

    d_copy.wait()
    g_copy.wait()
    u_copy.wait()

    def rank_block(b):
        t = meta[0, b]
        down = lax.dot_general(xv[b], dv[t], NT, preferred_element_type=F32)
        back = lax.dot_general(gv[b], uv[t], NT, preferred_element_type=F32)
        lp[b] = jnp.concatenate([down, back], axis=1)

    loop(blocks, rank_block)
    l_step(4)
    for r in (3, 5):
        w_copy(r).wait()
    loop(2, lambda i: event(i % 2, 2 * (1 - i % 2) + i // 2, 3, True))
    l_step(3)
    loop(2, lambda i: event(i % 2, 2 * (1 - i % 2) + 1, 3, True))
    l_step(2)
    loop(2, lambda i: event(i % 2, 2 * (i % 2) + i // 2, 3, False))
    l_step(1)
    loop(2, lambda i: event(i % 2, 2 * (i % 2) + 1, 3, False))
    for h in range(2):
        for dr in range(2):
            l_copy(dr, h, 1).wait_recv()
        v = lp[l_rows(0, h)] + lrb[0, h, 0] + lrb[1, h, 0]
        lall[l_rows(0, h)] = v.astype(BF16)
    for o in (4, 3, 5, 2, 6, 1, 7):
        gather_copy(o, zi).start()

    for r in (2, 6):
        w_copy(r).wait()
    loop(8, lambda i: event(i % 2, i // 2, 2, False))

    for o in range(1, Z):
        gather_copy(o, (zi - o + Z) % Z).wait_recv()

    def grads(k):
        b1, b2 = meta[1, k], meta[2, k]
        m1, m2 = meta[3, k].astype(F32), meta[4, k].astype(F32)
        rows = jnp.concatenate([lall[b1].astype(F32) * m1, lall[b2].astype(F32) * m2], axis=0).astype(BF16)
        xs = jnp.concatenate([xv[b1], xv[b2]], axis=0)
        gs = jnp.concatenate([gv[b1], gv[b2]], axis=0)
        return (
            lax.dot_general(rows[:, rank:], xs, TN, preferred_element_type=F32),
            lax.dot_general(rows[:, :rank], gs, TN, preferred_element_type=F32),
        )

    def pair_copy(j):
        return pltpu.make_async_remote_copy(
            src_ref=s1.at[j], dst_ref=r1.at[j], send_sem=s1s.at[j], recv_sem=s1r.at[j],
            device_id={"seq": seq_at(yi, xi, 1 - ci)}, device_id_type=MESH,
        )

    def for_sibling(i):
        j = X * Y - 1 - i
        ga, gb = grads(seq_at((yi + j // X) % Y, (xi + j % X) % X, 1 - ci))
        s1[j, :, :depth] = ga.astype(BF16)
        s1[j, :, depth:] = gb.astype(BF16)
        pair_copy(j).start()

    def a_copy(oy, ox):
        return pltpu.make_async_remote_copy(
            src_ref=sg.at[oy * X + ox, 0], dst_ref=ra.at[ox - 1, oy], send_sem=ras.at[ox - 1, oy], recv_sem=rar.at[ox - 1, oy],
            device_id={"seq": seq_at(yi, (xi + ox) % X, ci)}, device_id_type=MESH,
        )

    def b_copy(oy, ox):
        return pltpu.make_async_remote_copy(
            src_ref=sg.at[oy * X + ox, 1], dst_ref=rb.at[oy - 1, ox], send_sem=rbs.at[oy - 1, ox], recv_sem=rbr.at[oy - 1, ox],
            device_id={"seq": seq_at((yi + oy) % Y, xi, ci)}, device_id_type=MESH,
        )

    def a_last(o):
        return pltpu.make_async_remote_copy(
            src_ref=ta.at[o - 1], dst_ref=ra3.at[o - 1], send_sem=tas.at[o - 1], recv_sem=tar.at[o - 1],
            device_id={"seq": seq_at((yi + o) % Y, xi, ci)}, device_id_type=MESH,
        )

    def b_last(o):
        return pltpu.make_async_remote_copy(
            src_ref=tb.at[o - 1], dst_ref=rb3.at[o - 1], send_sem=tbs.at[o - 1], recv_sem=tbr.at[o - 1],
            device_id={"seq": seq_at(yi, (xi + o) % X, ci)}, device_id_type=MESH,
        )

    def for_pair(i):
        j = X * Y - 1 - i
        oy, ox = j // X, j % X
        ga, gb = grads(seq_at((yi + oy) % Y, (xi + ox) % X, ci))
        pair_copy(j).wait_recv()
        ga = (ga + r1[j, :, :depth].astype(F32)).astype(BF16)
        gb = (gb + r1[j, :, depth:].astype(F32)).astype(BF16)
        for h in range(2):
            sg[j, h, :, :depth] = ga[h * half : (h + 1) * half]
            sg[j, h, :, depth:] = gb[h * half : (h + 1) * half]

        @pl.when(ox > 0)
        def _():
            a_copy(oy, ox).start()

        @pl.when(oy > 0)
        def _():
            b_copy(oy, ox).start()

    loop(X * Y, for_sibling)
    loop(X * Y, for_pair)

    for r in (1, 7):
        w_copy(r).wait()
    loop(8, lambda i: event(i % 2, i // 2, 1, False))

    def branch_block(b):
        v = jnp.dot(lall[b][:, :rank], uv[meta[0, b]], preferred_element_type=F32)
        branch[b] = ADAPTER_SCALE * v

    loop(blocks, branch_block)

    for o in (2, 1, 3, 0):
        for p in range(1, 4):
            a_copy(o, p).wait_recv()
            b_copy(p, o).wait_recv()
        va, vb = sg[o * X, 0].astype(F32), sg[o, 1].astype(F32)
        for p in range(3):
            va = va + ra[p, o].astype(F32)
            vb = vb + rb[p, o].astype(F32)
        if o == 0:
            fin[0], fin[1] = va, vb
        else:
            ta[o - 1], tb[o - 1] = va.astype(BF16), vb.astype(BF16)
            a_last(o).start()
            b_last(o).start()

    def out_copy(q, i):
        target = seq_at((yi + q + 1) % Y, (xi + i // 2) % X, (ci + i) % C)
        return pltpu.make_async_remote_copy(
            src_ref=mix.at[target], dst_ref=out_h.at[si], send_sem=os.at[q, i], recv_sem=orr.at[q, i],
            device_id={"seq": target}, device_id_type=MESH,
        )

    def out_arrival(q, i):
        source = seq_at((yi + 2 * Y - q - 1) % Y, (xi + X - i // 2) % X, (ci + i) % C)
        return pltpu.make_async_remote_copy(
            src_ref=mix.at[source], dst_ref=out_h.at[source], send_sem=os.at[q, i], recv_sem=orr.at[q, i],
            device_id={"seq": source}, device_id_type=MESH,
        )

    self_copy = pltpu.make_async_copy(mix.at[si], out_h.at[si], loc)
    w_copy(0).wait()

    def finish(q):
        v = own(q, 0)
        for dr in range(2):
            z_copy(dr, q, 1).wait_recv()
        v = v + rbuf[0, q, 0].astype(F32) + rbuf[1, q, 0].astype(F32)
        at = pl.ds(rows_of(q), per)
        mix[at] = (v.reshape(per, blk, cols) + branch[at]).astype(BF16)

        def send(i):
            @pl.when(q * per + i != (CHUNKS - 1) * per)
            def _():
                out_copy(q, i).start()

        loop(per, send)

    loop(CHUNKS, finish)
    self_copy.start()

    for o in range(1, 4):
        a_last(o).wait_recv()
        b_last(o).wait_recv()
    for h, last in ((0, ra3), (1, rb3)):
        v = fin[h]
        for p in range(3):
            v = v + last[p].astype(F32)
        v = ADAPTER_SCALE * v
        ga_o[0, h * half : (h + 1) * half] = v[:, :depth]
        gb_o[0, h * half : (h + 1) * half] = v[:, depth:]

    def out_wait(n):
        @pl.when(n != (CHUNKS - 1) * per)
        def _():
            out_arrival(n // per, n % per).wait_recv()
            out_copy(n // per, n % per).wait_send()

    loop(blocks, out_wait)
    self_copy.wait()

    loop(4, lambda i: z_copy(i % 2, 2 * (i % 2) + i // 2, 4).wait_send())
    loop(24, lambda i: z_copy(i % 2, (i // 2) % 4, i // 8 + 1).wait_send())
    for dr in range(2):
        for h in range(2):
            for d in range(1, 5 if h == dr else 4):
                l_copy(dr, h, d).wait_send()
    for o in range(1, Z):
        gather_copy(o, zi).wait_send()
    loop(X * Y, lambda j: pair_copy(j).wait_send())
    for o in range(4):
        for p in range(1, 4):
            a_copy(o, p).wait_send()
            b_copy(p, o).wait_send()
    for o in range(1, 4):
        a_last(o).wait_send()
        b_last(o).wait_send()


def tables(trial_per_block, trial_slot_index):
    blocks = trial_per_block.shape[0]
    trials = trial_slot_index.shape[0]
    trial = trial_per_block[:, 0]
    numbers = jnp.arange(trials, dtype=jnp.int32)
    slot = jnp.sum(jnp.where(trial[:, None] == numbers[None, :], trial_slot_index[None, :], 0), axis=1)
    here = slot[None, :] == numbers[:, None]
    block = jnp.arange(blocks, dtype=jnp.int32)[None, :]
    first = jnp.min(jnp.where(here, block, blocks), axis=1)
    last = jnp.max(jnp.where(here, block, -1), axis=1)
    return jnp.stack([
        trial, jnp.minimum(first, blocks - 1), jnp.maximum(last, 0),
        (last >= 0).astype(jnp.int32), (last > first).astype(jnp.int32),
    ])


def local(x, g, trial_per_block, trial_slot_index, w, down, up):
    blocks = trial_per_block.shape[0]
    trials, depth, rank = down.shape
    cols = up.shape[2]
    blk = x.shape[0] // blocks
    half, wide = rank // 2, depth + cols
    chunk = x.shape[0] // CHUNKS
    hbm = pl.BlockSpec(memory_space=pl.ANY)
    vmem = pl.BlockSpec(memory_space=pltpu.VMEM)
    dma = pltpu.SemaphoreType.DMA
    out, ga, gb = pl.pallas_call(
        kernel,
        out_shape=(
            jax.ShapeDtypeStruct((SEQ, blk, cols), BF16),
            jax.ShapeDtypeStruct((1, rank, depth), F32),
            jax.ShapeDtypeStruct((1, rank, cols), F32),
        ),
        in_specs=[pl.BlockSpec(memory_space=pltpu.SMEM)] + [hbm] * 5,
        out_specs=(hbm, vmem, vmem),
        scratch_shapes=[
            pltpu.VMEM((blocks, blk, depth), BF16),
            pltpu.VMEM((blocks, blk, cols), BF16),
            pltpu.VMEM((Z, depth, cols), BF16),
            pltpu.VMEM((trials, rank, depth), BF16),
            pltpu.VMEM((trials, rank, cols), BF16),
            pltpu.VMEM((2, CHUNKS, 4, chunk, cols), BF16),
            pltpu.VMEM((2, CHUNKS, 4, chunk, cols), BF16),
            pltpu.VMEM((blocks, blk, 2 * rank), F32),
            pltpu.VMEM((2, 2, 4, 2, blk, 2 * rank), F32),
            pltpu.VMEM((2, 2, 4, 2, blk, 2 * rank), F32),
            pltpu.VMEM((blocks, blk, 2 * rank), BF16),
            pltpu.VMEM((X * Y, rank, wide), BF16),
            pltpu.VMEM((X * Y, rank, wide), BF16),
            pltpu.VMEM((X * Y, 2, half, wide), BF16),
            pltpu.VMEM((3, 4, half, wide), BF16),
            pltpu.VMEM((3, 4, half, wide), BF16),
            pltpu.VMEM((3, half, wide), BF16),
            pltpu.VMEM((3, half, wide), BF16),
            pltpu.VMEM((3, half, wide), BF16),
            pltpu.VMEM((3, half, wide), BF16),
            pltpu.VMEM((2, half, wide), F32),
            pltpu.VMEM((blocks, blk, cols), F32),
            pltpu.VMEM((blocks, blk, cols), BF16),
            dma((12,)),
            dma((2, CHUNKS, 4)), dma((2, CHUNKS, 4)),
            dma((2, 2, 4)), dma((2, 2, 4)),
            dma((Z - 1,)), dma((Z - 1,)),
            dma((X * Y,)), dma((X * Y,)),
            dma((3, 4)), dma((3, 4)), dma((3, 4)), dma((3, 4)),
            dma((3,)), dma((3,)), dma((3,)), dma((3,)),
            dma((CHUNKS, blocks // CHUNKS)), dma((CHUNKS, blocks // CHUNKS)),
            dma,
        ],
        compiler_params=pltpu.CompilerParams(collective_id=0, has_side_effects=True, vmem_limit_bytes=56 * 2**20),
    )(
        tables(trial_per_block, trial_slot_index),
        x.reshape(blocks, blk, depth), g.reshape(blocks, blk, cols), w, jnp.transpose(down, (0, 2, 1)), up,
    )
    return out.reshape(x.shape[0], cols), jnp.transpose(ga, (0, 2, 1)), gb


def solution(mesh):
    in_specs = (
        P("seq", "grp"),
        P("seq", "grp"),
        P("seq", None),
        P(),
        P("grp", None),
        P(None, "grp", None),
        P(None, None, "grp"),
    )
    out_specs = (P("seq", "grp"), P("seq", "grp", None), P("seq", None, "grp"))
    return jax.shard_map(local, mesh=mesh, in_specs=in_specs, out_specs=out_specs, check_vma=False)
```

```python
import jax
import jax.numpy as jnp
from jax import lax
from jax.experimental import pallas as pl
from jax.experimental.pallas import tpu as pltpu
from jax.sharding import PartitionSpec as P

ADAPTER_SCALE = 2.0
MESH = pl.DeviceIdType.MESH
F32, BF16 = jnp.float32, jnp.bfloat16
RANK_SENT = BF16
NT = (((1,), (1,)), ((), ()))
TN = (((0,), (0,)), ((), ()))
Z, Y, X, C = 8, 4, 4, 2
SEQ = Y * X * C
CHUNKS = 4


ORDER = (
    (2, 2), (0, 2), (2, 0), (1, 2), (3, 2), (2, 1), (2, 3), (1, 1),
    (1, 3), (3, 1), (3, 3), (0, 1), (0, 3), (1, 0), (3, 0), (0, 0),
)


def loop(n, body, unroll=1):
    lax.fori_loop(0, n, lambda i, c: (body(i), c)[1], 0, unroll=unroll)


def kernel(
    trial, slot, trial_row, x_h, g_h, w_h, d_h, u_h, out_h, ga_o, gb_o,
    tab_v, tab, xv, gv, wv, dv, uv, sbuf, rbuf, lp, lsb, lrb, lall, s1, r1, sg, rf, ra, ta, tb, ra3, rb3, fin, branch, mix,
    ld_sem, zs, zr, ls, lr, ags, agr, s1s, s1r, rfs, rfr, ras, rar, tas, tar, tbs, tbr, os, orr, loc,
):
    zi, si = lax.axis_index("grp"), lax.axis_index("seq")
    ci, xi, yi = si % C, (si // C) % X, si // (C * X)
    blocks, blk, depth = xv.shape
    cols = gv.shape[2]
    rank = dv.shape[1]
    half = rank // 2
    per = blocks // CHUNKS
    wide = depth + cols

    def seq_at(y, x, c):
        return (y * X + x) * C + c

    barrier = pltpu.get_barrier_semaphore()
    loop(SEQ - 1, lambda o: pl.semaphore_signal(barrier, inc=1, device_id={"seq": (si + o + 1) % SEQ}, device_id_type=MESH))
    loop(Z - 1, lambda o: pl.semaphore_signal(barrier, inc=1, device_id={"grp": (zi + o + 1) % Z}, device_id_type=MESH))

    def w_copy(r):
        at = pl.multiple_of(((zi + r) % Z) * cols, cols)
        return pltpu.make_async_copy(w_h.at[:, pl.ds(at, cols)], wv.at[r], ld_sem.at[r])

    x_copy = pltpu.make_async_copy(x_h, xv, ld_sem.at[8])
    g_copy = pltpu.make_async_copy(g_h, gv, ld_sem.at[9])
    d_copy = pltpu.make_async_copy(d_h, dv, ld_sem.at[10])
    u_copy = pltpu.make_async_copy(u_h, uv, ld_sem.at[11])
    x_copy.start()
    w_copy(4).start()
    d_copy.start()
    g_copy.start()
    u_copy.start()
    for r in (3, 5, 2, 6, 1, 7, 0):
        w_copy(r).start()

    def rows_of(q):
        return ((yi + q + 1) % Y) * per

    def own(q, r):
        rows = xv[pl.ds(rows_of(q), per)].reshape(per * blk, depth)
        return jnp.dot(rows, wv[r], preferred_element_type=F32)

    def z_copy(dr, q, d):
        return pltpu.make_async_remote_copy(
            src_ref=sbuf.at[dr, q, d - 1], dst_ref=rbuf.at[dr, q, d - 1],
            send_sem=zs.at[dr, q, d - 1], recv_sem=zr.at[dr, q, d - 1],
            device_id={"grp": (zi + 1 - 2 * dr + Z) % Z}, device_id_type=MESH,
        )

    def event(dr, q, d, first):
        v = own(q, ((1 - 2 * dr) * d + Z) % Z)
        if not first:
            z_copy(dr, q, d + 1).wait_recv()
            v = v + rbuf[dr, q, d].astype(F32)
        sbuf[dr, q, d - 1] = v.astype(BF16)
        z_copy(dr, q, d).start()

    def l_copy(o):
        return pltpu.make_async_remote_copy(
            src_ref=lsb.at[pl.ds(((zi + o) % Z) * 4, 4)], dst_ref=lrb.at[o - 1], send_sem=ls.at[o - 1], recv_sem=lr.at[o - 1],
            device_id={"grp": (zi + o) % Z}, device_id_type=MESH,
        )

    def gather_copy(o, source):
        at = pl.ds(source * 4, 4)
        return pltpu.make_async_remote_copy(
            src_ref=lall.at[at], dst_ref=lall.at[at], send_sem=ags.at[o - 1], recv_sem=agr.at[o - 1],
            device_id={"grp": (zi + o) % Z}, device_id_type=MESH,
        )

    count = slot.shape[0]
    slot_row = jnp.zeros((1, blocks), jnp.int32)
    for t in range(count):
        slot_row = jnp.where(trial_row[...] == t, slot[t], slot_row)
    here = jnp.broadcast_to(slot_row, (count, blocks)) == lax.broadcasted_iota(jnp.int32, (count, blocks), 0)
    number = lax.broadcasted_iota(jnp.int32, (count, blocks), 1)
    first = jnp.min(jnp.where(here, number, blocks), axis=1, keepdims=True)
    last = jnp.max(jnp.where(here, number, -1), axis=1, keepdims=True)
    lane = lax.broadcasted_iota(jnp.int32, tab_v.shape, 1)
    row = jnp.where(lane == 0, jnp.minimum(first, blocks - 1), jnp.maximum(last, 0))
    row = jnp.where(lane == 2, (last >= 0).astype(jnp.int32), row)
    tab_v[...] = jnp.where(lane == 3, (last > first).astype(jnp.int32), row)
    tab_copy = pltpu.make_async_copy(tab_v, tab, ld_sem.at[12])
    tab_copy.start()

    x_copy.wait()
    w_copy(4).wait()
    pl.semaphore_wait(barrier, SEQ - 1 + Z - 1)

    loop(4, lambda i: event(i % 2, 2 * (i % 2) + i // 2, 4, True), 2)

    d_copy.wait()
    g_copy.wait()
    u_copy.wait()

    def rank_block(b):
        t = trial[b]
        down = lax.dot_general(xv[b], dv[t], NT, preferred_element_type=F32)
        back = lax.dot_general(gv[b], uv[t], NT, preferred_element_type=F32)
        v = jnp.concatenate([down, back], axis=1)
        lp[b] = v
        lsb[b] = v.astype(lsb.dtype)

    loop(blocks, rank_block, 8)
    for o in (4, 3, 5, 2, 6, 1, 7):
        l_copy(o).start()
    for r in (3, 5):
        w_copy(r).wait()
    loop(4, lambda i: event(i % 2, 2 * (1 - i % 2) + i // 2, 3, True), 2)
    mine = pl.ds(zi * 4, 4)
    v = lp[mine]
    for o in range(1, Z):
        l_copy(o).wait_recv()
        v = v + lrb[o - 1].astype(F32)
    lall[mine] = v.astype(BF16)
    for o in (4, 3, 5, 2, 6, 1, 7):
        gather_copy(o, zi).start()
    loop(4, lambda i: event(i % 2, 2 * (i % 2) + i // 2, 3, False), 2)

    for o in range(1, Z):
        gather_copy(o, (zi - o + Z) % Z).wait_recv()

    def grads(k):
        b1, b2 = tab[k, 0], tab[k, 1]
        m1, m2 = tab[k, 2].astype(F32), tab[k, 3].astype(F32)
        rows = jnp.concatenate([lall[b1].astype(F32) * m1, lall[b2].astype(F32) * m2], axis=0).astype(BF16)
        xs = jnp.concatenate([xv[b1], xv[b2]], axis=0)
        gs = jnp.concatenate([gv[b1], gv[b2]], axis=0)
        return (
            lax.dot_general(rows[:, rank:], xs, TN, preferred_element_type=F32),
            lax.dot_general(rows[:, :rank], gs, TN, preferred_element_type=F32),
        )

    def pair_copy(j):
        return pltpu.make_async_remote_copy(
            src_ref=s1.at[j], dst_ref=r1.at[j], send_sem=s1s.at[j], recv_sem=s1r.at[j],
            device_id={"seq": seq_at(yi, xi, 1 - ci)}, device_id_type=MESH,
        )

    def for_sibling(i):
        oy, ox = ORDER[i]
        j = oy * X + ox
        ga, gb = grads(seq_at((yi + oy) % Y, (xi + ox) % X, 1 - ci))
        s1[j, :, :depth] = ga.astype(BF16)
        s1[j, :, depth:] = gb.astype(BF16)
        pair_copy(j).start()

    def slot_of(h, p, o):
        return o * X + p if h == 0 else p * X + o

    def along(h, p):
        return {"seq": seq_at(yi, (xi + p) % X, ci) if h == 0 else seq_at((yi + p) % Y, xi, ci)}

    def far_copy(h, w, o):
        return pltpu.make_async_remote_copy(
            src_ref=sg.at[slot_of(h, 2, o), h, pl.ds(w * half // 2, half // 2)], dst_ref=rf.at[h, w, o],
            send_sem=rfs.at[h, w, o], recv_sem=rfr.at[h, w, o], device_id=along(h, 1 + 2 * w), device_id_type=MESH,
        )

    def near_copy(h, w, o):
        return pltpu.make_async_remote_copy(
            src_ref=sg.at[slot_of(h, 1 + 2 * w, o), h], dst_ref=ra.at[h, w, o],
            send_sem=ras.at[h, w, o], recv_sem=rar.at[h, w, o], device_id=along(h, 1 + 2 * w), device_id_type=MESH,
        )

    def a_last(o):
        return pltpu.make_async_remote_copy(
            src_ref=ta.at[o - 1], dst_ref=ra3.at[o - 1], send_sem=tas.at[o - 1], recv_sem=tar.at[o - 1],
            device_id={"seq": seq_at((yi + o) % Y, xi, ci)}, device_id_type=MESH,
        )

    def b_last(o):
        return pltpu.make_async_remote_copy(
            src_ref=tb.at[o - 1], dst_ref=rb3.at[o - 1], send_sem=tbs.at[o - 1], recv_sem=tbr.at[o - 1],
            device_id={"seq": seq_at(yi, (xi + o) % X, ci)}, device_id_type=MESH,
        )

    def for_pair(i):
        oy, ox = ORDER[i]
        j = oy * X + ox
        ga, gb = grads(seq_at((yi + oy) % Y, (xi + ox) % X, ci))
        pair_copy(j).wait_recv()
        for h, p, o in ((0, ox, oy), (1, oy, ox)):
            if p % 2:
                far_copy(h, p // 2, o).wait_recv()
            for w in range(2):
                at = h * half + w * half // 2
                rows = slice(at, at + half // 2)
                va = ga[rows] + r1[j, rows, :depth].astype(F32)
                vb = gb[rows] + r1[j, rows, depth:].astype(F32)
                if p == 1 + 2 * w:
                    va = va + rf[h, w, o, :, :depth].astype(F32)
                    vb = vb + rf[h, w, o, :, depth:].astype(F32)
                to = slice(w * half // 2, (w + 1) * half // 2)
                sg[j, h, to, :depth] = va.astype(BF16)
                sg[j, h, to, depth:] = vb.astype(BF16)
            if p == 2:
                far_copy(h, 0, o).start()
                far_copy(h, 1, o).start()
            elif p:
                near_copy(h, p // 2, o).start()

    tab_copy.wait()
    for r in (2, 6, 1, 7):
        w_copy(r).wait()

    for i in range(8):
        for_sibling(2 * i)
        for_sibling(2 * i + 1)
        if i >= 4:
            for_pair(2 * (i - 4))
            for_pair(2 * (i - 4) + 1)
        event(i % 2, i // 2, 2, False)
    for i in range(8):
        for_pair(8 + i)
        event(i % 2, i // 2, 1, False)

    def branch_block(b):
        v = jnp.dot(lall[b][:, :rank], uv[trial[b]], preferred_element_type=F32)
        branch[b] = ADAPTER_SCALE * v

    loop(blocks, branch_block, 8)

    def column(o):
        for w in range(2):
            near_copy(0, w, o).wait_recv()
            near_copy(1, w, o).wait_recv()
        va, vb = (
            sg[slot_of(h, 0, o), h].astype(F32) + ra[h, 0, o].astype(F32) + ra[h, 1, o].astype(F32) for h in range(2)
        )
        if o == 0:
            fin[0], fin[1] = va, vb
        else:
            ta[o - 1], tb[o - 1] = va.astype(BF16), vb.astype(BF16)
            a_last(o).start()
            b_last(o).start()

    def out_copy(q, i):
        target = seq_at((yi + q + 1) % Y, (xi + i // 2) % X, (ci + i) % C)
        return pltpu.make_async_remote_copy(
            src_ref=mix.at[target], dst_ref=out_h.at[si], send_sem=os.at[q, i], recv_sem=orr.at[q, i],
            device_id={"seq": target}, device_id_type=MESH,
        )

    def out_arrival(q, i):
        source = seq_at((yi + 2 * Y - q - 1) % Y, (xi + X - i // 2) % X, (ci + i) % C)
        return pltpu.make_async_remote_copy(
            src_ref=mix.at[source], dst_ref=out_h.at[source], send_sem=os.at[q, i], recv_sem=orr.at[q, i],
            device_id={"seq": source}, device_id_type=MESH,
        )

    self_copy = pltpu.make_async_copy(mix.at[si], out_h.at[si], loc)
    w_copy(0).wait()

    def finish(q):
        v = own(q, 0)
        for dr in range(2):
            z_copy(dr, q, 1).wait_recv()
        v = v + rbuf[0, q, 0].astype(F32) + rbuf[1, q, 0].astype(F32)
        at = pl.ds(rows_of(q), per)
        mix[at] = (v.reshape(per, blk, cols) + branch[at]).astype(BF16)

        def send(i):
            @pl.when(q * per + i != (CHUNKS - 1) * per)
            def _():
                out_copy(q, i).start()

        loop(per, send)

    column(2)
    column(1)
    finish(0)
    column(3)
    column(0)
    finish(1)
    finish(2)
    finish(3)
    self_copy.start()

    for o in range(1, 4):
        a_last(o).wait_recv()
        b_last(o).wait_recv()
    for h, last in ((0, ra3), (1, rb3)):
        v = fin[h]
        for p in range(3):
            v = v + last[p].astype(F32)
        v = ADAPTER_SCALE * v
        ga_o[0, h * half : (h + 1) * half] = v[:, :depth]
        gb_o[0, h * half : (h + 1) * half] = v[:, depth:]

    def out_wait(n):
        @pl.when(n != (CHUNKS - 1) * per)
        def _():
            out_arrival(n // per, n % per).wait_recv()
            out_copy(n // per, n % per).wait_send()

    loop(blocks, out_wait)
    self_copy.wait()

    loop(4, lambda i: z_copy(i % 2, 2 * (i % 2) + i // 2, 4).wait_send())
    loop(24, lambda i: z_copy(i % 2, (i // 2) % 4, i // 8 + 1).wait_send())
    for o in range(1, Z):
        l_copy(o).wait_send()
        gather_copy(o, zi).wait_send()
    loop(X * Y, lambda j: pair_copy(j).wait_send())
    for o in range(4):
        for w in range(2):
            for h in range(2):
                far_copy(h, w, o).wait_send()
                near_copy(h, w, o).wait_send()
    for o in range(1, 4):
        a_last(o).wait_send()
        b_last(o).wait_send()


def place(out, ga, gb, out_o, ga_o, gb_o):
    out_o[...] = out[...]
    ga_o[...] = ga[...]
    gb_o[...] = gb[...]


def local(x, g, trial_per_block, trial_slot_index, w, down, up):
    blocks = trial_per_block.shape[0]
    trials, depth, rank = down.shape
    cols = up.shape[2]
    blk = x.shape[0] // blocks
    half, wide = rank // 2, depth + cols
    chunk = x.shape[0] // CHUNKS
    hbm = pl.BlockSpec(memory_space=pl.ANY)
    vmem = pl.BlockSpec(memory_space=pltpu.VMEM)
    dma = pltpu.SemaphoreType.DMA
    out, ga, gb = pl.pallas_call(
        kernel,
        out_shape=(
            jax.ShapeDtypeStruct((SEQ, blk, cols), BF16),
            jax.ShapeDtypeStruct((1, rank, depth), F32),
            jax.ShapeDtypeStruct((1, rank, cols), F32),
        ),
        in_specs=[pl.BlockSpec(memory_space=pltpu.SMEM)] * 2 + [vmem] + [hbm] * 5,
        out_specs=(hbm, vmem, vmem),
        scratch_shapes=[
            pltpu.VMEM((trials, 128), jnp.int32),
            pltpu.SMEM((trials, 128), jnp.int32),
            pltpu.VMEM((blocks, blk, depth), BF16),
            pltpu.VMEM((blocks, blk, cols), BF16),
            pltpu.VMEM((Z, depth, cols), BF16),
            pltpu.VMEM((trials, rank, depth), BF16),
            pltpu.VMEM((trials, rank, cols), BF16),
            pltpu.VMEM((2, CHUNKS, 4, chunk, cols), BF16),
            pltpu.VMEM((2, CHUNKS, 4, chunk, cols), BF16),
            pltpu.VMEM((blocks, blk, 2 * rank), F32),
            pltpu.VMEM((blocks, blk, 2 * rank), RANK_SENT),
            pltpu.VMEM((Z - 1, 4, blk, 2 * rank), RANK_SENT),
            pltpu.VMEM((blocks, blk, 2 * rank), BF16),
            pltpu.VMEM((X * Y, rank, wide), BF16),
            pltpu.VMEM((X * Y, rank, wide), BF16),
            pltpu.VMEM((X * Y, 2, half, wide), BF16),
            pltpu.VMEM((2, 2, 4, half // 2, wide), BF16),
            pltpu.VMEM((2, 2, 4, half, wide), BF16),
            pltpu.VMEM((3, half, wide), BF16),
            pltpu.VMEM((3, half, wide), BF16),
            pltpu.VMEM((3, half, wide), BF16),
            pltpu.VMEM((3, half, wide), BF16),
            pltpu.VMEM((2, half, wide), F32),
            pltpu.VMEM((blocks, blk, cols), F32),
            pltpu.VMEM((blocks, blk, cols), BF16),
            dma((13,)),
            dma((2, CHUNKS, 4)), dma((2, CHUNKS, 4)),
            dma((Z - 1,)), dma((Z - 1,)),
            dma((Z - 1,)), dma((Z - 1,)),
            dma((X * Y,)), dma((X * Y,)),
            dma((2, 2, 4)), dma((2, 2, 4)), dma((2, 2, 4)), dma((2, 2, 4)),
            dma((3,)), dma((3,)), dma((3,)), dma((3,)),
            dma((CHUNKS, blocks // CHUNKS)), dma((CHUNKS, blocks // CHUNKS)),
            dma,
        ],
        compiler_params=pltpu.CompilerParams(collective_id=0, has_side_effects=True, vmem_limit_bytes=56 * 2**20),
    )(
        trial_per_block.reshape(blocks), trial_slot_index, trial_per_block.reshape(1, blocks),
        x.reshape(blocks, blk, depth), g.reshape(blocks, blk, cols), w, jnp.transpose(down, (0, 2, 1)), up,
    )
    out, ga, gb = pl.pallas_call(
        place,
        out_shape=tuple(jax.ShapeDtypeStruct(v.shape, v.dtype) for v in (out, ga, gb)),
        in_specs=[vmem] * 3,
        out_specs=(vmem,) * 3,
    )(out, ga, gb)
    return out.reshape(x.shape[0], cols), jnp.transpose(ga, (0, 2, 1)), gb


def solution(mesh):
    in_specs = (
        P("seq", "grp"),
        P("seq", "grp"),
        P("seq", None),
        P(),
        P("grp", None),
        P(None, "grp", None),
        P(None, None, "grp"),
    )
    out_specs = (P("seq", "grp"), P("seq", "grp", None), P("seq", None, "grp"))
    return jax.shard_map(local, mesh=mesh, in_specs=in_specs, out_specs=out_specs, check_vma=False)
```

```python
import jax
import jax.numpy as jnp
from jax import lax
from jax.experimental import pallas as pl
from jax.experimental.pallas import tpu as pltpu
from jax.sharding import PartitionSpec as P

ADAPTER_SCALE = 2.0
MESH = pl.DeviceIdType.MESH
F32, BF16 = jnp.float32, jnp.bfloat16
RANK_SENT = BF16
NT = (((1,), (1,)), ((), ()))
TN = (((0,), (0,)), ((), ()))
Z, Y, X, C = 8, 4, 4, 2
SEQ = Y * X * C
CHUNKS = 4


ORDER = (
    (2, 2), (0, 2), (2, 0), (1, 2), (3, 2), (2, 1), (2, 3), (1, 1),
    (1, 3), (3, 1), (3, 3), (0, 1), (0, 3), (1, 0), (3, 0), (0, 0),
)


def loop(n, body, unroll=1):
    lax.fori_loop(0, n, lambda i, c: (body(i), c)[1], 0, unroll=unroll)


def kernel(
    trial, slot, trial_row, x_h, g_h, w_h, d_h, u_h, out_h, ga_o, gb_o,
    tab_v, tab, xv, gv, wv, dv, uv, sbuf, rbuf, lp, lsb, lrb, lall, s1, r1, sg, rf, ra, ta, tb, ra3, rb3, fin, branch, mix, ga_v, gb_v,
    ld_sem, zs, zr, ls, lr, ags, agr, s1s, s1r, rfs, rfr, ras, rar, tas, tar, tbs, tbr, os, orr, loc,
):
    zi, si = lax.axis_index("grp"), lax.axis_index("seq")
    ci, xi, yi = si % C, (si // C) % X, si // (C * X)
    blocks, blk, depth = xv.shape
    cols = gv.shape[2]
    rank = dv.shape[1]
    half = rank // 2
    per = blocks // CHUNKS
    wide = depth + cols

    def seq_at(y, x, c):
        return (y * X + x) * C + c

    barrier = pltpu.get_barrier_semaphore()
    loop(SEQ - 1, lambda o: pl.semaphore_signal(barrier, inc=1, device_id={"seq": (si + o + 1) % SEQ}, device_id_type=MESH))
    loop(Z - 1, lambda o: pl.semaphore_signal(barrier, inc=1, device_id={"grp": (zi + o + 1) % Z}, device_id_type=MESH))

    def w_copy(r):
        at = pl.multiple_of(((zi + r) % Z) * cols, cols)
        return pltpu.make_async_copy(w_h.at[:, pl.ds(at, cols)], wv.at[r], ld_sem.at[r])

    x_copy = pltpu.make_async_copy(x_h, xv, ld_sem.at[8])
    g_copy = pltpu.make_async_copy(g_h, gv, ld_sem.at[9])
    d_copy = pltpu.make_async_copy(d_h, dv, ld_sem.at[10])
    u_copy = pltpu.make_async_copy(u_h, uv, ld_sem.at[11])
    x_copy.start()
    w_copy(4).start()
    d_copy.start()
    g_copy.start()
    u_copy.start()
    for r in (3, 5, 2, 6, 1, 7, 0):
        w_copy(r).start()

    def rows_of(q):
        return ((yi + q + 1) % Y) * per

    def own(q, r):
        rows = xv[pl.ds(rows_of(q), per)].reshape(per * blk, depth)
        return jnp.dot(rows, wv[r], preferred_element_type=F32)

    def z_copy(dr, q, d):
        return pltpu.make_async_remote_copy(
            src_ref=sbuf.at[dr, q, d - 1], dst_ref=rbuf.at[dr, q, d - 1],
            send_sem=zs.at[dr, q, d - 1], recv_sem=zr.at[dr, q, d - 1],
            device_id={"grp": (zi + 1 - 2 * dr + Z) % Z}, device_id_type=MESH,
        )

    def events(places, d, first):
        sums = [own(q, ((1 - 2 * dr) * d + Z) % Z) for dr, q in enumerate(places)]
        if not first:
            for dr, q in enumerate(places):
                z_copy(dr, q, d + 1).wait_recv()
            sums = [v + rbuf[dr, q, d].astype(F32) for v, (dr, q) in zip(sums, enumerate(places))]
        for v, (dr, q) in zip(sums, enumerate(places)):
            sbuf[dr, q, d - 1] = v.astype(BF16)
        for dr, q in enumerate(places):
            z_copy(dr, q, d).start()

    def l_copy(o):
        return pltpu.make_async_remote_copy(
            src_ref=lsb.at[pl.ds(((zi + o) % Z) * 4, 4)], dst_ref=lrb.at[o - 1], send_sem=ls.at[o - 1], recv_sem=lr.at[o - 1],
            device_id={"grp": (zi + o) % Z}, device_id_type=MESH,
        )

    def gather_copy(o, source):
        at = pl.ds(source * 4, 4)
        return pltpu.make_async_remote_copy(
            src_ref=lall.at[at], dst_ref=lall.at[at], send_sem=ags.at[o - 1], recv_sem=agr.at[o - 1],
            device_id={"grp": (zi + o) % Z}, device_id_type=MESH,
        )

    count = slot.shape[0]
    slot_row = jnp.zeros((1, blocks), jnp.int32)
    for t in range(count):
        slot_row = jnp.where(trial_row[...] == t, slot[t], slot_row)
    here = jnp.broadcast_to(slot_row, (count, blocks)) == lax.broadcasted_iota(jnp.int32, (count, blocks), 0)
    number = lax.broadcasted_iota(jnp.int32, (count, blocks), 1)
    first = jnp.min(jnp.where(here, number, blocks), axis=1, keepdims=True)
    last = jnp.max(jnp.where(here, number, -1), axis=1, keepdims=True)
    lane = lax.broadcasted_iota(jnp.int32, tab_v.shape, 1)
    row = jnp.where(lane == 0, jnp.minimum(first, blocks - 1), jnp.maximum(last, 0))
    row = jnp.where(lane == 2, (last >= 0).astype(jnp.int32), row)
    tab_v[...] = jnp.where(lane == 3, (last > first).astype(jnp.int32), row)
    tab_copy = pltpu.make_async_copy(tab_v, tab, ld_sem.at[12])
    tab_copy.start()

    x_copy.wait()
    w_copy(4).wait()
    pl.semaphore_wait(barrier, SEQ - 1 + Z - 1)

    for i in range(2):
        events((i, 2 + i), 4, True)

    d_copy.wait()
    g_copy.wait()
    u_copy.wait()

    def rank_block(b):
        t = trial[b]
        down = lax.dot_general(xv[b], dv[t], NT, preferred_element_type=F32)
        back = lax.dot_general(gv[b], uv[t], NT, preferred_element_type=F32)
        v = jnp.concatenate([down, back], axis=1)
        lp[b] = v
        lsb[b] = v.astype(lsb.dtype)

    loop(blocks, rank_block, 8)
    for o in (4, 3, 5, 2, 6, 1, 7):
        l_copy(o).start()
    for r in (3, 5):
        w_copy(r).wait()
    for i in range(2):
        events((2 + i, i), 3, True)
    mine = pl.ds(zi * 4, 4)
    v = lp[mine]
    for o in range(1, Z):
        l_copy(o).wait_recv()
        v = v + lrb[o - 1].astype(F32)
    lall[mine] = v.astype(BF16)
    for o in (4, 3, 5, 2, 6, 1, 7):
        gather_copy(o, zi).start()
    for i in range(2):
        events((i, 2 + i), 3, False)

    for o in range(1, Z):
        gather_copy(o, (zi - o + Z) % Z).wait_recv()

    def grads(k):
        b1, b2 = tab[k, 0], tab[k, 1]
        m1, m2 = tab[k, 2].astype(F32), tab[k, 3].astype(F32)
        rows = jnp.concatenate([lall[b1].astype(F32) * m1, lall[b2].astype(F32) * m2], axis=0).astype(BF16)
        xs = jnp.concatenate([xv[b1], xv[b2]], axis=0)
        gs = jnp.concatenate([gv[b1], gv[b2]], axis=0)
        return (
            lax.dot_general(rows[:, rank:], xs, TN, preferred_element_type=F32),
            lax.dot_general(rows[:, :rank], gs, TN, preferred_element_type=F32),
        )

    def pair_copy(j):
        return pltpu.make_async_remote_copy(
            src_ref=s1.at[j], dst_ref=r1.at[j], send_sem=s1s.at[j], recv_sem=s1r.at[j],
            device_id={"seq": seq_at(yi, xi, 1 - ci)}, device_id_type=MESH,
        )

    def for_sibling(turns):
        places = [ORDER[i] for i in turns]
        made = [grads(seq_at((yi + oy) % Y, (xi + ox) % X, 1 - ci)) for oy, ox in places]
        for (oy, ox), (ga, gb) in zip(places, made):
            s1[oy * X + ox, :, :depth] = ga.astype(BF16)
            s1[oy * X + ox, :, depth:] = gb.astype(BF16)
        for oy, ox in places:
            pair_copy(oy * X + ox).start()

    def slot_of(h, p, o):
        return o * X + p if h == 0 else p * X + o

    def along(h, p):
        return {"seq": seq_at(yi, (xi + p) % X, ci) if h == 0 else seq_at((yi + p) % Y, xi, ci)}

    def far_copy(h, w, o):
        return pltpu.make_async_remote_copy(
            src_ref=sg.at[slot_of(h, 2, o), h, pl.ds(w * half // 2, half // 2)], dst_ref=rf.at[h, w, o],
            send_sem=rfs.at[h, w, o], recv_sem=rfr.at[h, w, o], device_id=along(h, 1 + 2 * w), device_id_type=MESH,
        )

    def near_copy(h, w, o):
        return pltpu.make_async_remote_copy(
            src_ref=sg.at[slot_of(h, 1 + 2 * w, o), h], dst_ref=ra.at[h, w, o],
            send_sem=ras.at[h, w, o], recv_sem=rar.at[h, w, o], device_id=along(h, 1 + 2 * w), device_id_type=MESH,
        )

    def a_last(o):
        return pltpu.make_async_remote_copy(
            src_ref=ta.at[o - 1], dst_ref=ra3.at[o - 1], send_sem=tas.at[o - 1], recv_sem=tar.at[o - 1],
            device_id={"seq": seq_at((yi + o) % Y, xi, ci)}, device_id_type=MESH,
        )

    def b_last(o):
        return pltpu.make_async_remote_copy(
            src_ref=tb.at[o - 1], dst_ref=rb3.at[o - 1], send_sem=tbs.at[o - 1], recv_sem=tbr.at[o - 1],
            device_id={"seq": seq_at(yi, (xi + o) % X, ci)}, device_id_type=MESH,
        )

    def for_pair(turns):
        places = [ORDER[i] for i in turns]
        parts = [(j, h, p, o) for j, oy, ox in [(y * X + x, y, x) for y, x in places] for h, p, o in ((0, ox, oy), (1, oy, ox))]
        made = {oy * X + ox: grads(seq_at((yi + oy) % Y, (xi + ox) % X, ci)) for oy, ox in places}
        for j in made:
            pair_copy(j).wait_recv()
        for j, h, p, o in parts:
            if p % 2:
                far_copy(h, p // 2, o).wait_recv()
        for j, h, p, o in parts:
            ga, gb = made[j]
            for w in range(2):
                at = h * half + w * half // 2
                rows = slice(at, at + half // 2)
                va = ga[rows] + r1[j, rows, :depth].astype(F32)
                vb = gb[rows] + r1[j, rows, depth:].astype(F32)
                if p == 1 + 2 * w:
                    va = va + rf[h, w, o, :, :depth].astype(F32)
                    vb = vb + rf[h, w, o, :, depth:].astype(F32)
                to = slice(w * half // 2, (w + 1) * half // 2)
                sg[j, h, to, :depth] = va.astype(BF16)
                sg[j, h, to, depth:] = vb.astype(BF16)
        for j, h, p, o in parts:
            if p == 2:
                far_copy(h, 0, o).start()
                far_copy(h, 1, o).start()
            elif p:
                near_copy(h, p // 2, o).start()

    tab_copy.wait()
    for r in (2, 6, 1, 7):
        w_copy(r).wait()

    for i in range(8):
        for_sibling(range(2 * i, 2 * i + 2))
    for i in range(4):
        for_pair(range(2 * i, 2 * i + 2))
        events((i, i), 2, False)
    for i in range(4):
        for_pair(range(8 + 2 * i, 10 + 2 * i))
        events((i, i), 1, False)

    def branch_block(b):
        v = jnp.dot(lall[b][:, :rank], uv[trial[b]], preferred_element_type=F32)
        branch[b] = ADAPTER_SCALE * v

    loop(blocks, branch_block, 8)

    def column(o):
        for w in range(2):
            near_copy(0, w, o).wait_recv()
            near_copy(1, w, o).wait_recv()
        va, vb = (
            sg[slot_of(h, 0, o), h].astype(F32) + ra[h, 0, o].astype(F32) + ra[h, 1, o].astype(F32) for h in range(2)
        )
        if o == 0:
            fin[0], fin[1] = va, vb
        else:
            ta[o - 1], tb[o - 1] = va.astype(BF16), vb.astype(BF16)
            a_last(o).start()
            b_last(o).start()

    def out_copy(q, i):
        target = seq_at((yi + q + 1) % Y, (xi + i // 2) % X, (ci + i) % C)
        return pltpu.make_async_remote_copy(
            src_ref=mix.at[target], dst_ref=out_h.at[si], send_sem=os.at[q, i], recv_sem=orr.at[q, i],
            device_id={"seq": target}, device_id_type=MESH,
        )

    def out_arrival(q, i):
        source = seq_at((yi + 2 * Y - q - 1) % Y, (xi + X - i // 2) % X, (ci + i) % C)
        return pltpu.make_async_remote_copy(
            src_ref=mix.at[source], dst_ref=out_h.at[source], send_sem=os.at[q, i], recv_sem=orr.at[q, i],
            device_id={"seq": source}, device_id_type=MESH,
        )

    self_copy = pltpu.make_async_copy(mix.at[si], out_h.at[si], loc.at[0])
    w_copy(0).wait()

    def finish(q):
        v = own(q, 0)
        for dr in range(2):
            z_copy(dr, q, 1).wait_recv()
        v = v + rbuf[0, q, 0].astype(F32) + rbuf[1, q, 0].astype(F32)
        at = pl.ds(rows_of(q), per)
        mix[at] = (v.reshape(per, blk, cols) + branch[at]).astype(BF16)

        def send(i):
            @pl.when(q * per + i != (CHUNKS - 1) * per)
            def _():
                out_copy(q, i).start()

        loop(per, send)

    column(2)
    column(1)
    finish(0)
    column(3)
    column(0)
    finish(1)
    finish(2)
    finish(3)
    self_copy.start()

    for o in range(1, 4):
        a_last(o).wait_recv()
        b_last(o).wait_recv()
    for h, last in ((0, ra3), (1, rb3)):
        v = fin[h]
        for p in range(3):
            v = v + last[p].astype(F32)
        v = ADAPTER_SCALE * v
        ga_v[h * half : (h + 1) * half] = v[:, :depth]
        gb_v[h * half : (h + 1) * half] = v[:, depth:]
    ga_copy = pltpu.make_async_copy(ga_v, ga_o.at[0], loc.at[1])
    gb_copy = pltpu.make_async_copy(gb_v, gb_o.at[0], loc.at[2])
    ga_copy.start()
    gb_copy.start()

    loop(4, lambda i: z_copy(i % 2, 2 * (i % 2) + i // 2, 4).wait_send())
    loop(24, lambda i: z_copy(i % 2, (i // 2) % 4, i // 8 + 1).wait_send())
    for o in range(1, Z):
        l_copy(o).wait_send()
        gather_copy(o, zi).wait_send()
    loop(X * Y, lambda j: pair_copy(j).wait_send())
    for o in range(4):
        for w in range(2):
            for h in range(2):
                far_copy(h, w, o).wait_send()
                near_copy(h, w, o).wait_send()
    for o in range(1, 4):
        a_last(o).wait_send()
        b_last(o).wait_send()

    def out_wait(n):
        @pl.when(n != (CHUNKS - 1) * per)
        def _():
            out_copy(n // per, n % per).wait_send()
            out_arrival(n // per, n % per).wait_recv()

    loop(blocks, out_wait)
    self_copy.wait()
    ga_copy.wait()
    gb_copy.wait()


def place(out, ga, gb, out_o, ga_o, gb_o):
    out_o[...] = out[...]
    ga_o[...] = ga[...]
    gb_o[...] = gb[...]


def local(x, g, trial_per_block, trial_slot_index, w, down, up):
    blocks = trial_per_block.shape[0]
    trials, depth, rank = down.shape
    cols = up.shape[2]
    blk = x.shape[0] // blocks
    half, wide = rank // 2, depth + cols
    chunk = x.shape[0] // CHUNKS
    hbm = pl.BlockSpec(memory_space=pl.ANY)
    vmem = pl.BlockSpec(memory_space=pltpu.VMEM)
    dma = pltpu.SemaphoreType.DMA
    out, ga, gb = pl.pallas_call(
        kernel,
        out_shape=(
            jax.ShapeDtypeStruct((SEQ, blk, cols), BF16),
            jax.ShapeDtypeStruct((1, rank, depth), F32),
            jax.ShapeDtypeStruct((1, rank, cols), F32),
        ),
        in_specs=[pl.BlockSpec(memory_space=pltpu.SMEM)] * 2 + [vmem] + [hbm] * 5,
        out_specs=(hbm,) * 3,
        scratch_shapes=[
            pltpu.VMEM((trials, 128), jnp.int32),
            pltpu.SMEM((trials, 128), jnp.int32),
            pltpu.VMEM((blocks, blk, depth), BF16),
            pltpu.VMEM((blocks, blk, cols), BF16),
            pltpu.VMEM((Z, depth, cols), BF16),
            pltpu.VMEM((trials, rank, depth), BF16),
            pltpu.VMEM((trials, rank, cols), BF16),
            pltpu.VMEM((2, CHUNKS, 4, chunk, cols), BF16),
            pltpu.VMEM((2, CHUNKS, 4, chunk, cols), BF16),
            pltpu.VMEM((blocks, blk, 2 * rank), F32),
            pltpu.VMEM((blocks, blk, 2 * rank), RANK_SENT),
            pltpu.VMEM((Z - 1, 4, blk, 2 * rank), RANK_SENT),
            pltpu.VMEM((blocks, blk, 2 * rank), BF16),
            pltpu.VMEM((X * Y, rank, wide), BF16),
            pltpu.VMEM((X * Y, rank, wide), BF16),
            pltpu.VMEM((X * Y, 2, half, wide), BF16),
            pltpu.VMEM((2, 2, 4, half // 2, wide), BF16),
            pltpu.VMEM((2, 2, 4, half, wide), BF16),
            pltpu.VMEM((3, half, wide), BF16),
            pltpu.VMEM((3, half, wide), BF16),
            pltpu.VMEM((3, half, wide), BF16),
            pltpu.VMEM((3, half, wide), BF16),
            pltpu.VMEM((2, half, wide), F32),
            pltpu.VMEM((blocks, blk, cols), F32),
            pltpu.VMEM((blocks, blk, cols), BF16),
            pltpu.VMEM((rank, depth), F32),
            pltpu.VMEM((rank, cols), F32),
            dma((13,)),
            dma((2, CHUNKS, 4)), dma((2, CHUNKS, 4)),
            dma((Z - 1,)), dma((Z - 1,)),
            dma((Z - 1,)), dma((Z - 1,)),
            dma((X * Y,)), dma((X * Y,)),
            dma((2, 2, 4)), dma((2, 2, 4)), dma((2, 2, 4)), dma((2, 2, 4)),
            dma((3,)), dma((3,)), dma((3,)), dma((3,)),
            dma((CHUNKS, blocks // CHUNKS)), dma((CHUNKS, blocks // CHUNKS)),
            dma((3,)),
        ],
        compiler_params=pltpu.CompilerParams(collective_id=0, has_side_effects=True, vmem_limit_bytes=56 * 2**20),
    )(
        trial_per_block.reshape(blocks), trial_slot_index, trial_per_block.reshape(1, blocks),
        x.reshape(blocks, blk, depth), g.reshape(blocks, blk, cols), w, jnp.transpose(down, (0, 2, 1)), up,
    )
    out, ga, gb = pl.pallas_call(
        place,
        out_shape=tuple(jax.ShapeDtypeStruct(v.shape, v.dtype) for v in (out, ga, gb)),
        in_specs=[vmem] * 3,
        out_specs=(vmem,) * 3,
    )(out, ga, gb)
    return out.reshape(x.shape[0], cols), jnp.transpose(ga, (0, 2, 1)), gb


def solution(mesh):
    in_specs = (
        P("seq", "grp"),
        P("seq", "grp"),
        P("seq", None),
        P(),
        P("grp", None),
        P(None, "grp", None),
        P(None, None, "grp"),
    )
    out_specs = (P("seq", "grp"), P("seq", "grp", None), P("seq", None, "grp"))
    return jax.shard_map(local, mesh=mesh, in_specs=in_specs, out_specs=out_specs, check_vma=False)
```

```python
import jax
import jax.numpy as jnp
from jax import lax
from jax.experimental import pallas as pl
from jax.experimental.pallas import tpu as pltpu
from jax.sharding import PartitionSpec as P

ADAPTER_SCALE = 2.0
MESH = pl.DeviceIdType.MESH
F32, BF16 = jnp.float32, jnp.bfloat16
RANK_SENT = BF16
NT = (((1,), (1,)), ((), ()))
TN = (((0,), (0,)), ((), ()))
Z, Y, X, C = 8, 4, 4, 2
SEQ = Y * X * C
CHUNKS = 4


ORDER = (
    (2, 2), (0, 2), (2, 0), (1, 2), (3, 2), (2, 1), (2, 3), (1, 1),
    (1, 3), (3, 1), (3, 3), (0, 1), (0, 3), (1, 0), (3, 0), (0, 0),
)


def loop(n, body, unroll=1):
    lax.fori_loop(0, n, lambda i, c: (body(i), c)[1], 0, unroll=unroll)


def kernel(
    trial, slot, trial_row, x_h, g_h, w_h, d_h, u_h, out_h, ga_o, gb_o,
    tab_v, tab, xv, gv, wv, dv, uv, sbuf, rbuf, lp, lsb, lrb, lall, s1, r1, sg, rf, ra, ta, tb, ra3, rb3, fin, branch, mix, ga_v, gb_v,
    ld_sem, zs, zr, ls, lr, ags, agr, s1s, s1r, rfs, rfr, ras, rar, tas, tar, tbs, tbr, os, orr, loc,
):
    zi, si = lax.axis_index("grp"), lax.axis_index("seq")
    ci, xi, yi = si % C, (si // C) % X, si // (C * X)
    blocks, blk, depth = xv.shape
    cols = gv.shape[2]
    rank = dv.shape[1]
    half = rank // 2
    per = blocks // CHUNKS
    wide = depth + cols

    def seq_at(y, x, c):
        return (y * X + x) * C + c

    barrier = pltpu.get_barrier_semaphore()
    loop(SEQ - 1, lambda o: pl.semaphore_signal(barrier, inc=1, device_id={"seq": (si + o + 1) % SEQ}, device_id_type=MESH))
    loop(Z - 1, lambda o: pl.semaphore_signal(barrier, inc=1, device_id={"grp": (zi + o + 1) % Z}, device_id_type=MESH))

    def w_copy(r):
        at = pl.multiple_of(((zi + r) % Z) * cols, cols)
        return pltpu.make_async_copy(w_h.at[:, pl.ds(at, cols)], wv.at[r], ld_sem.at[r])

    x_copy = pltpu.make_async_copy(x_h, xv, ld_sem.at[8])
    g_copy = pltpu.make_async_copy(g_h, gv, ld_sem.at[9])
    d_copy = pltpu.make_async_copy(d_h, dv, ld_sem.at[10])
    u_copy = pltpu.make_async_copy(u_h, uv, ld_sem.at[11])
    x_copy.start()
    w_copy(4).start()
    d_copy.start()
    g_copy.start()
    u_copy.start()
    for r in (3, 5, 2, 6, 1, 7, 0):
        w_copy(r).start()

    def rows_of(q):
        return ((yi + q + 1) % Y) * per

    def own(q, r):
        rows = xv[pl.ds(rows_of(q), per)].reshape(per * blk, depth)
        return jnp.dot(rows, wv[r], preferred_element_type=F32)

    def z_copy(dr, q, d):
        return pltpu.make_async_remote_copy(
            src_ref=sbuf.at[dr, q, d - 1], dst_ref=rbuf.at[dr, q, d - 1],
            send_sem=zs.at[dr, q, d - 1], recv_sem=zr.at[dr, q, d - 1],
            device_id={"grp": (zi + 1 - 2 * dr + Z) % Z}, device_id_type=MESH,
        )

    def events(places, d, first):
        sums = [own(q, ((1 - 2 * dr) * d + Z) % Z) for dr, q in enumerate(places)]
        if not first:
            for dr, q in enumerate(places):
                z_copy(dr, q, d + 1).wait_recv()
            sums = [v + rbuf[dr, q, d].astype(F32) for v, (dr, q) in zip(sums, enumerate(places))]
        for v, (dr, q) in zip(sums, enumerate(places)):
            sbuf[dr, q, d - 1] = v.astype(BF16)
        for dr, q in enumerate(places):
            z_copy(dr, q, d).start()

    def l_copy(o):
        return pltpu.make_async_remote_copy(
            src_ref=lsb.at[pl.ds(((zi + o) % Z) * 4, 4)], dst_ref=lrb.at[o - 1], send_sem=ls.at[o - 1], recv_sem=lr.at[o - 1],
            device_id={"grp": (zi + o) % Z}, device_id_type=MESH,
        )

    def gather_copy(o, source):
        at = pl.ds(source * 4, 4)
        return pltpu.make_async_remote_copy(
            src_ref=lall.at[at], dst_ref=lall.at[at], send_sem=ags.at[o - 1], recv_sem=agr.at[o - 1],
            device_id={"grp": (zi + o) % Z}, device_id_type=MESH,
        )

    count = slot.shape[0]
    slot_row = jnp.zeros((1, blocks), jnp.int32)
    for t in range(count):
        slot_row = jnp.where(trial_row[...] == t, slot[t], slot_row)
    here = jnp.broadcast_to(slot_row, (count, blocks)) == lax.broadcasted_iota(jnp.int32, (count, blocks), 0)
    number = lax.broadcasted_iota(jnp.int32, (count, blocks), 1)
    first = jnp.min(jnp.where(here, number, blocks), axis=1, keepdims=True)
    last = jnp.max(jnp.where(here, number, -1), axis=1, keepdims=True)
    lane = lax.broadcasted_iota(jnp.int32, tab_v.shape, 1)
    row = jnp.where(lane == 0, jnp.minimum(first, blocks - 1), jnp.maximum(last, 0))
    row = jnp.where(lane == 2, (last >= 0).astype(jnp.int32), row)
    tab_v[...] = jnp.where(lane == 3, (last > first).astype(jnp.int32), row)
    tab_copy = pltpu.make_async_copy(tab_v, tab, ld_sem.at[12])
    tab_copy.start()

    x_copy.wait()
    w_copy(4).wait()
    for q in range(CHUNKS):
        sbuf[q // 2, q, 3] = own(q, 4).astype(BF16)
    pl.semaphore_wait(barrier, SEQ - 1 + Z - 1)
    for q in (0, 2, 1, 3):
        z_copy(q // 2, q, 4).start()

    d_copy.wait()
    g_copy.wait()
    u_copy.wait()

    def rank_block(b):
        t = trial[b]
        down = lax.dot_general(xv[b], dv[t], NT, preferred_element_type=F32)
        back = lax.dot_general(gv[b], uv[t], NT, preferred_element_type=F32)
        v = jnp.concatenate([down, back], axis=1)
        lp[b] = v
        lsb[b] = v.astype(lsb.dtype)

    loop(blocks, rank_block, 8)
    for o in (4, 3, 5, 2, 6, 1, 7):
        l_copy(o).start()
    for r in (3, 5):
        w_copy(r).wait()
    for i in range(2):
        events((2 + i, i), 3, True)
    mine = pl.ds(zi * 4, 4)
    v = lp[mine]
    for o in range(1, Z):
        l_copy(o).wait_recv()
        v = v + lrb[o - 1].astype(F32)
    lall[mine] = v.astype(BF16)
    for o in (4, 3, 5, 2, 6, 1, 7):
        gather_copy(o, zi).start()
    for i in range(2):
        events((i, 2 + i), 3, False)

    for o in range(1, Z):
        gather_copy(o, (zi - o + Z) % Z).wait_recv()

    def grads(k):
        b1, b2 = tab[k, 0], tab[k, 1]
        m1, m2 = tab[k, 2].astype(F32), tab[k, 3].astype(F32)
        rows = jnp.concatenate([lall[b1].astype(F32) * m1, lall[b2].astype(F32) * m2], axis=0).astype(BF16)
        xs = jnp.concatenate([xv[b1], xv[b2]], axis=0)
        gs = jnp.concatenate([gv[b1], gv[b2]], axis=0)
        return (
            lax.dot_general(rows[:, rank:], xs, TN, preferred_element_type=F32),
            lax.dot_general(rows[:, :rank], gs, TN, preferred_element_type=F32),
        )

    def pair_copy(j):
        return pltpu.make_async_remote_copy(
            src_ref=s1.at[j], dst_ref=r1.at[j], send_sem=s1s.at[j], recv_sem=s1r.at[j],
            device_id={"seq": seq_at(yi, xi, 1 - ci)}, device_id_type=MESH,
        )

    def for_sibling(turns):
        places = [ORDER[i] for i in turns]
        made = [grads(seq_at((yi + oy) % Y, (xi + ox) % X, 1 - ci)) for oy, ox in places]
        for (oy, ox), (ga, gb) in zip(places, made):
            s1[oy * X + ox, :, :depth] = ga.astype(BF16)
            s1[oy * X + ox, :, depth:] = gb.astype(BF16)
        for oy, ox in places:
            pair_copy(oy * X + ox).start()

    def slot_of(h, p, o):
        return o * X + p if h == 0 else p * X + o

    def along(h, p):
        return {"seq": seq_at(yi, (xi + p) % X, ci) if h == 0 else seq_at((yi + p) % Y, xi, ci)}

    def far_copy(h, w, o):
        return pltpu.make_async_remote_copy(
            src_ref=sg.at[slot_of(h, 2, o), h, pl.ds(w * half // 2, half // 2)], dst_ref=rf.at[h, w, o],
            send_sem=rfs.at[h, w, o], recv_sem=rfr.at[h, w, o], device_id=along(h, 1 + 2 * w), device_id_type=MESH,
        )

    def near_copy(h, w, o):
        return pltpu.make_async_remote_copy(
            src_ref=sg.at[slot_of(h, 1 + 2 * w, o), h], dst_ref=ra.at[h, w, o],
            send_sem=ras.at[h, w, o], recv_sem=rar.at[h, w, o], device_id=along(h, 1 + 2 * w), device_id_type=MESH,
        )

    def a_last(o):
        return pltpu.make_async_remote_copy(
            src_ref=ta.at[o - 1], dst_ref=ra3.at[o - 1], send_sem=tas.at[o - 1], recv_sem=tar.at[o - 1],
            device_id={"seq": seq_at((yi + o) % Y, xi, ci)}, device_id_type=MESH,
        )

    def b_last(o):
        return pltpu.make_async_remote_copy(
            src_ref=tb.at[o - 1], dst_ref=rb3.at[o - 1], send_sem=tbs.at[o - 1], recv_sem=tbr.at[o - 1],
            device_id={"seq": seq_at(yi, (xi + o) % X, ci)}, device_id_type=MESH,
        )

    def for_pair(turns):
        places = [ORDER[i] for i in turns]
        parts = [(j, h, p, o) for j, oy, ox in [(y * X + x, y, x) for y, x in places] for h, p, o in ((0, ox, oy), (1, oy, ox))]
        made = {oy * X + ox: grads(seq_at((yi + oy) % Y, (xi + ox) % X, ci)) for oy, ox in places}
        for j in made:
            pair_copy(j).wait_recv()
        for j, h, p, o in parts:
            if p % 2:
                far_copy(h, p // 2, o).wait_recv()
        for j, h, p, o in parts:
            ga, gb = made[j]
            for w in range(2):
                at = h * half + w * half // 2
                rows = slice(at, at + half // 2)
                va = ga[rows] + r1[j, rows, :depth].astype(F32)
                vb = gb[rows] + r1[j, rows, depth:].astype(F32)
                if p == 1 + 2 * w:
                    va = va + rf[h, w, o, :, :depth].astype(F32)
                    vb = vb + rf[h, w, o, :, depth:].astype(F32)
                to = slice(w * half // 2, (w + 1) * half // 2)
                sg[j, h, to, :depth] = va.astype(BF16)
                sg[j, h, to, depth:] = vb.astype(BF16)
        for j, h, p, o in parts:
            if p == 2:
                far_copy(h, 0, o).start()
                far_copy(h, 1, o).start()
            elif p:
                near_copy(h, p // 2, o).start()

    tab_copy.wait()
    for r in (2, 6, 1, 7):
        w_copy(r).wait()

    for i in range(8):
        for_sibling(range(2 * i, 2 * i + 2))
    for i in range(4):
        events((i, i), 2, False)
        for_pair(range(2 * i, 2 * i + 2))
    for i in range(4):
        events((i, i), 1, False)
        for_pair(range(8 + 2 * i, 10 + 2 * i))

    def branch_block(b):
        v = jnp.dot(lall[b][:, :rank], uv[trial[b]], preferred_element_type=F32)
        branch[b] = ADAPTER_SCALE * v

    loop(blocks, branch_block, 8)

    def column(o):
        for w in range(2):
            near_copy(0, w, o).wait_recv()
            near_copy(1, w, o).wait_recv()
        va, vb = (
            sg[slot_of(h, 0, o), h].astype(F32) + ra[h, 0, o].astype(F32) + ra[h, 1, o].astype(F32) for h in range(2)
        )
        if o == 0:
            fin[0], fin[1] = va, vb
        else:
            ta[o - 1], tb[o - 1] = va.astype(BF16), vb.astype(BF16)
            a_last(o).start()
            b_last(o).start()

    def out_copy(q, i):
        target = seq_at((yi + q + 1) % Y, (xi + i // 2) % X, (ci + i) % C)
        return pltpu.make_async_remote_copy(
            src_ref=mix.at[target], dst_ref=out_h.at[si], send_sem=os.at[q, i], recv_sem=orr.at[q, i],
            device_id={"seq": target}, device_id_type=MESH,
        )

    def out_arrival(q, i):
        source = seq_at((yi + 2 * Y - q - 1) % Y, (xi + X - i // 2) % X, (ci + i) % C)
        return pltpu.make_async_remote_copy(
            src_ref=mix.at[source], dst_ref=out_h.at[source], send_sem=os.at[q, i], recv_sem=orr.at[q, i],
            device_id={"seq": source}, device_id_type=MESH,
        )

    self_copy = pltpu.make_async_copy(mix.at[si], out_h.at[si], loc.at[0])
    w_copy(0).wait()

    def finish(q):
        v = own(q, 0)
        for dr in range(2):
            z_copy(dr, q, 1).wait_recv()
        v = v + rbuf[0, q, 0].astype(F32) + rbuf[1, q, 0].astype(F32)
        at = pl.ds(rows_of(q), per)
        mix[at] = (v.reshape(per, blk, cols) + branch[at]).astype(BF16)

        def send(i):
            @pl.when(q * per + i != (CHUNKS - 1) * per)
            def _():
                out_copy(q, i).start()

        loop(per, send)

    column(2)
    column(1)
    finish(0)
    column(3)
    column(0)
    finish(1)
    finish(2)
    finish(3)
    self_copy.start()

    for o in range(1, 4):
        a_last(o).wait_recv()
        b_last(o).wait_recv()
    for h, last in ((0, ra3), (1, rb3)):
        v = fin[h]
        for p in range(3):
            v = v + last[p].astype(F32)
        v = ADAPTER_SCALE * v
        ga_v[h * half : (h + 1) * half] = v[:, :depth]
        gb_v[h * half : (h + 1) * half] = v[:, depth:]
    ga_copy = pltpu.make_async_copy(ga_v, ga_o.at[0], loc.at[1])
    gb_copy = pltpu.make_async_copy(gb_v, gb_o.at[0], loc.at[2])
    ga_copy.start()
    gb_copy.start()

    loop(4, lambda i: z_copy(i % 2, 2 * (i % 2) + i // 2, 4).wait_send())
    loop(24, lambda i: z_copy(i % 2, (i // 2) % 4, i // 8 + 1).wait_send())
    for o in range(1, Z):
        l_copy(o).wait_send()
        gather_copy(o, zi).wait_send()
    loop(X * Y, lambda j: pair_copy(j).wait_send())
    for o in range(4):
        for w in range(2):
            for h in range(2):
                far_copy(h, w, o).wait_send()
                near_copy(h, w, o).wait_send()
    for o in range(1, 4):
        a_last(o).wait_send()
        b_last(o).wait_send()

    def out_wait(n):
        @pl.when(n != (CHUNKS - 1) * per)
        def _():
            out_copy(n // per, n % per).wait_send()
            out_arrival(n // per, n % per).wait_recv()

    loop(blocks, out_wait)
    self_copy.wait()
    ga_copy.wait()
    gb_copy.wait()


def place(out, ga, gb, out_o, ga_o, gb_o, out_v, ga_v, gb_v, get, put):
    ways = ((out, out_v, out_o), (ga, ga_v, ga_o), (gb, gb_v, gb_o))
    gets = [pltpu.make_async_copy(a, v, get.at[i]) for i, (a, v, b) in enumerate(ways)]
    puts = [pltpu.make_async_copy(v, b, put.at[i]) for i, (a, v, b) in enumerate(ways)]
    for copy in gets:
        copy.start()
    for i in range(3):
        gets[i].wait()
        puts[i].start()
    for copy in puts:
        copy.wait()


def local(x, g, trial_per_block, trial_slot_index, w, down, up):
    blocks = trial_per_block.shape[0]
    trials, depth, rank = down.shape
    cols = up.shape[2]
    blk = x.shape[0] // blocks
    half, wide = rank // 2, depth + cols
    chunk = x.shape[0] // CHUNKS
    hbm = pl.BlockSpec(memory_space=pl.ANY)
    vmem = pl.BlockSpec(memory_space=pltpu.VMEM)
    dma = pltpu.SemaphoreType.DMA
    out, ga, gb = pl.pallas_call(
        kernel,
        out_shape=(
            jax.ShapeDtypeStruct((SEQ, blk, cols), BF16),
            jax.ShapeDtypeStruct((1, rank, depth), F32),
            jax.ShapeDtypeStruct((1, rank, cols), F32),
        ),
        in_specs=[pl.BlockSpec(memory_space=pltpu.SMEM)] * 2 + [vmem] + [hbm] * 5,
        out_specs=(hbm,) * 3,
        scratch_shapes=[
            pltpu.VMEM((trials, 128), jnp.int32),
            pltpu.SMEM((trials, 128), jnp.int32),
            pltpu.VMEM((blocks, blk, depth), BF16),
            pltpu.VMEM((blocks, blk, cols), BF16),
            pltpu.VMEM((Z, depth, cols), BF16),
            pltpu.VMEM((trials, rank, depth), BF16),
            pltpu.VMEM((trials, rank, cols), BF16),
            pltpu.VMEM((2, CHUNKS, 4, chunk, cols), BF16),
            pltpu.VMEM((2, CHUNKS, 4, chunk, cols), BF16),
            pltpu.VMEM((blocks, blk, 2 * rank), F32),
            pltpu.VMEM((blocks, blk, 2 * rank), RANK_SENT),
            pltpu.VMEM((Z - 1, 4, blk, 2 * rank), RANK_SENT),
            pltpu.VMEM((blocks, blk, 2 * rank), BF16),
            pltpu.VMEM((X * Y, rank, wide), BF16),
            pltpu.VMEM((X * Y, rank, wide), BF16),
            pltpu.VMEM((X * Y, 2, half, wide), BF16),
            pltpu.VMEM((2, 2, 4, half // 2, wide), BF16),
            pltpu.VMEM((2, 2, 4, half, wide), BF16),
            pltpu.VMEM((3, half, wide), BF16),
            pltpu.VMEM((3, half, wide), BF16),
            pltpu.VMEM((3, half, wide), BF16),
            pltpu.VMEM((3, half, wide), BF16),
            pltpu.VMEM((2, half, wide), F32),
            pltpu.VMEM((blocks, blk, cols), F32),
            pltpu.VMEM((blocks, blk, cols), BF16),
            pltpu.VMEM((rank, depth), F32),
            pltpu.VMEM((rank, cols), F32),
            dma((13,)),
            dma((2, CHUNKS, 4)), dma((2, CHUNKS, 4)),
            dma((Z - 1,)), dma((Z - 1,)),
            dma((Z - 1,)), dma((Z - 1,)),
            dma((X * Y,)), dma((X * Y,)),
            dma((2, 2, 4)), dma((2, 2, 4)), dma((2, 2, 4)), dma((2, 2, 4)),
            dma((3,)), dma((3,)), dma((3,)), dma((3,)),
            dma((CHUNKS, blocks // CHUNKS)), dma((CHUNKS, blocks // CHUNKS)),
            dma((3,)),
        ],
        compiler_params=pltpu.CompilerParams(collective_id=0, has_side_effects=True, vmem_limit_bytes=56 * 2**20),
    )(
        trial_per_block.reshape(blocks), trial_slot_index, trial_per_block.reshape(1, blocks),
        x.reshape(blocks, blk, depth), g.reshape(blocks, blk, cols), w, jnp.transpose(down, (0, 2, 1)), up,
    )
    out, ga, gb = pl.pallas_call(
        place,
        out_shape=tuple(jax.ShapeDtypeStruct(v.shape, v.dtype) for v in (out, ga, gb)),
        in_specs=[hbm] * 3,
        out_specs=(hbm,) * 3,
        scratch_shapes=[pltpu.VMEM(v.shape, v.dtype) for v in (out, ga, gb)] + [dma((3,)), dma((3,))],
    )(out, ga, gb)
    return out.reshape(x.shape[0], cols), jnp.transpose(ga, (0, 2, 1)), gb


def solution(mesh):
    in_specs = (
        P("seq", "grp"),
        P("seq", "grp"),
        P("seq", None),
        P(),
        P("grp", None),
        P(None, "grp", None),
        P(None, None, "grp"),
    )
    out_specs = (P("seq", "grp"), P("seq", "grp", None), P("seq", None, "grp"))
    return jax.shard_map(local, mesh=mesh, in_specs=in_specs, out_specs=out_specs, check_vma=False)
```

```python
import jax
import jax.numpy as jnp
from jax import lax
from jax.experimental import pallas as pl
from jax.experimental.pallas import tpu as pltpu
from jax.sharding import PartitionSpec as P

ADAPTER_SCALE = 2.0
MESH = pl.DeviceIdType.MESH
F32, BF16 = jnp.float32, jnp.bfloat16
RANK_SENT = BF16
NT = (((1,), (1,)), ((), ()))
TN = (((0,), (0,)), ((), ()))
Z, Y, X, C = 8, 4, 4, 2
SEQ = Y * X * C
CHUNKS = 4


ORDER = (
    (2, 2), (0, 2), (2, 0), (1, 2), (3, 2), (2, 1), (2, 3), (1, 1),
    (1, 3), (3, 1), (3, 3), (0, 1), (0, 3), (1, 0), (3, 0), (0, 0),
)


def loop(n, body, unroll=1):
    lax.fori_loop(0, n, lambda i, c: (body(i), c)[1], 0, unroll=unroll)


def kernel(
    trial, slot, trial_row, x_h, g_h, w_h, d_h, u_h, out_h, ga_o, gb_o,
    tab_v, tab, xv, gv, wv, dv, uv, sbuf, rbuf, lp, lsb, lrb, lall, s1, r1, sg, rf, ra, ta, tb, ra3, rb3, fin, branch, mix, ga_v, gb_v,
    ld_sem, zs, zr, ls, lr, ags, agr, s1s, s1r, rfs, rfr, ras, rar, tas, tar, tbs, tbr, os, orr, loc,
):
    zi, si = lax.axis_index("grp"), lax.axis_index("seq")
    ci, xi, yi = si % C, (si // C) % X, si // (C * X)
    blocks, blk, depth = xv.shape
    cols = gv.shape[2]
    rank = dv.shape[1]
    half = rank // 2
    per = blocks // CHUNKS
    wide = depth + cols

    def seq_at(y, x, c):
        return (y * X + x) * C + c

    barrier = pltpu.get_barrier_semaphore()
    loop(SEQ - 1, lambda o: pl.semaphore_signal(barrier, inc=1, device_id={"seq": (si + o + 1) % SEQ}, device_id_type=MESH))
    loop(Z - 1, lambda o: pl.semaphore_signal(barrier, inc=1, device_id={"grp": (zi + o + 1) % Z}, device_id_type=MESH))

    def w_copy(r):
        at = pl.multiple_of(((zi + r) % Z) * cols, cols)
        return pltpu.make_async_copy(w_h.at[:, pl.ds(at, cols)], wv.at[r], ld_sem.at[r])

    x_copy = pltpu.make_async_copy(x_h, xv, ld_sem.at[8])
    g_copy = pltpu.make_async_copy(g_h, gv, ld_sem.at[9])
    d_copy = pltpu.make_async_copy(d_h, dv, ld_sem.at[10])
    u_copy = pltpu.make_async_copy(u_h, uv, ld_sem.at[11])
    x_copy.start()
    w_copy(4).start()
    d_copy.start()
    g_copy.start()
    u_copy.start()
    for r in (3, 5, 2, 6, 1, 7, 0):
        w_copy(r).start()

    def rows_of(q):
        return ((yi + q + 1) % Y) * per

    def own(q, r):
        rows = xv[pl.ds(rows_of(q), per)].reshape(per * blk, depth)
        return jnp.dot(rows, wv[r], preferred_element_type=F32)

    def z_copy(dr, q, d):
        return pltpu.make_async_remote_copy(
            src_ref=sbuf.at[dr, q, d - 1], dst_ref=rbuf.at[dr, q, d - 1],
            send_sem=zs.at[dr, q, d - 1], recv_sem=zr.at[dr, q, d - 1],
            device_id={"grp": (zi + 1 - 2 * dr + Z) % Z}, device_id_type=MESH,
        )

    def events(places, d, first):
        sums = [own(q, ((1 - 2 * dr) * d + Z) % Z) for dr, q in enumerate(places)]
        if not first:
            for dr, q in enumerate(places):
                z_copy(dr, q, d + 1).wait_recv()
            sums = [v + rbuf[dr, q, d].astype(F32) for v, (dr, q) in zip(sums, enumerate(places))]
        for v, (dr, q) in zip(sums, enumerate(places)):
            sbuf[dr, q, d - 1] = v.astype(BF16)
        for dr, q in enumerate(places):
            z_copy(dr, q, d).start()

    def l_copy(o):
        return pltpu.make_async_remote_copy(
            src_ref=lsb.at[pl.ds(((zi + o) % Z) * 4, 4)], dst_ref=lrb.at[o - 1], send_sem=ls.at[o - 1], recv_sem=lr.at[o - 1],
            device_id={"grp": (zi + o) % Z}, device_id_type=MESH,
        )

    def gather_copy(o, source):
        at = pl.ds(source * 4, 4)
        return pltpu.make_async_remote_copy(
            src_ref=lall.at[at], dst_ref=lall.at[at], send_sem=ags.at[o - 1], recv_sem=agr.at[o - 1],
            device_id={"grp": (zi + o) % Z}, device_id_type=MESH,
        )

    count = slot.shape[0]
    slot_row = jnp.zeros((1, blocks), jnp.int32)
    for t in range(count):
        slot_row = jnp.where(trial_row[...] == t, slot[t], slot_row)
    here = jnp.broadcast_to(slot_row, (count, blocks)) == lax.broadcasted_iota(jnp.int32, (count, blocks), 0)
    number = lax.broadcasted_iota(jnp.int32, (count, blocks), 1)
    first = jnp.min(jnp.where(here, number, blocks), axis=1, keepdims=True)
    last = jnp.max(jnp.where(here, number, -1), axis=1, keepdims=True)
    lane = lax.broadcasted_iota(jnp.int32, tab_v.shape, 1)
    row = jnp.where(lane == 0, jnp.minimum(first, blocks - 1), jnp.maximum(last, 0))
    row = jnp.where(lane == 2, (last >= 0).astype(jnp.int32), row)
    tab_v[...] = jnp.where(lane == 3, (last > first).astype(jnp.int32), row)
    tab_copy = pltpu.make_async_copy(tab_v, tab, ld_sem.at[12])
    tab_copy.start()

    x_copy.wait()
    w_copy(4).wait()
    for q in range(CHUNKS):
        sbuf[q // 2, q, 3] = own(q, 4).astype(BF16)
    pl.semaphore_wait(barrier, SEQ - 1 + Z - 1)
    for q in (0, 2, 1, 3):
        z_copy(q // 2, q, 4).start()

    d_copy.wait()
    g_copy.wait()
    u_copy.wait()

    def rank_sums(o):
        made = []
        for n in range(4):
            b = ((zi + o) % Z) * 4 + n
            t = trial[b]
            down = lax.dot_general(xv[b], dv[t], NT, preferred_element_type=F32)
            back = lax.dot_general(gv[b], uv[t], NT, preferred_element_type=F32)
            made.append(jnp.concatenate([down, back], axis=1))
        return made

    for o in (4, 3, 5, 2, 6, 1, 7):
        for n, v in enumerate(rank_sums(o)):
            lsb[((zi + o) % Z) * 4 + n] = v.astype(RANK_SENT)
        l_copy(o).start()
    for n, v in enumerate(rank_sums(0)):
        lp[n] = v
    for r in (3, 5):
        w_copy(r).wait()
    for i in range(2):
        events((2 + i, i), 3, True)
    mine = pl.ds(zi * 4, 4)
    v = lp[...]
    for o in range(1, Z):
        l_copy(o).wait_recv()
        v = v + lrb[o - 1].astype(F32)
    lall[mine] = v.astype(BF16)
    for o in (4, 3, 5, 2, 6, 1, 7):
        gather_copy(o, zi).start()
    for i in range(2):
        events((i, 2 + i), 3, False)

    for o in range(1, Z):
        gather_copy(o, (zi - o + Z) % Z).wait_recv()

    def grads(k):
        b1, b2 = tab[k, 0], tab[k, 1]
        m1, m2 = tab[k, 2].astype(F32), tab[k, 3].astype(F32)
        rows = jnp.concatenate([lall[b1].astype(F32) * m1, lall[b2].astype(F32) * m2], axis=0).astype(BF16)
        xs = jnp.concatenate([xv[b1], xv[b2]], axis=0)
        gs = jnp.concatenate([gv[b1], gv[b2]], axis=0)
        return (
            lax.dot_general(rows[:, rank:], xs, TN, preferred_element_type=F32),
            lax.dot_general(rows[:, :rank], gs, TN, preferred_element_type=F32),
        )

    def pair_copy(j):
        return pltpu.make_async_remote_copy(
            src_ref=s1.at[j], dst_ref=r1.at[j], send_sem=s1s.at[j], recv_sem=s1r.at[j],
            device_id={"seq": seq_at(yi, xi, 1 - ci)}, device_id_type=MESH,
        )

    def for_sibling(turns):
        places = [ORDER[i] for i in turns]
        made = [grads(seq_at((yi + oy) % Y, (xi + ox) % X, 1 - ci)) for oy, ox in places]
        for (oy, ox), (ga, gb) in zip(places, made):
            s1[oy * X + ox, :, :depth] = ga.astype(BF16)
            s1[oy * X + ox, :, depth:] = gb.astype(BF16)
        for oy, ox in places:
            pair_copy(oy * X + ox).start()

    def slot_of(h, p, o):
        return o * X + p if h == 0 else p * X + o

    def along(h, p):
        return {"seq": seq_at(yi, (xi + p) % X, ci) if h == 0 else seq_at((yi + p) % Y, xi, ci)}

    def far_copy(h, w, o):
        return pltpu.make_async_remote_copy(
            src_ref=sg.at[slot_of(h, 2, o), h, pl.ds(w * half // 2, half // 2)], dst_ref=rf.at[h, w, o],
            send_sem=rfs.at[h, w, o], recv_sem=rfr.at[h, w, o], device_id=along(h, 1 + 2 * w), device_id_type=MESH,
        )

    def near_copy(h, w, o):
        return pltpu.make_async_remote_copy(
            src_ref=sg.at[slot_of(h, 1 + 2 * w, o), h], dst_ref=ra.at[h, w, o],
            send_sem=ras.at[h, w, o], recv_sem=rar.at[h, w, o], device_id=along(h, 1 + 2 * w), device_id_type=MESH,
        )

    def a_last(o):
        return pltpu.make_async_remote_copy(
            src_ref=ta.at[o - 1], dst_ref=ra3.at[o - 1], send_sem=tas.at[o - 1], recv_sem=tar.at[o - 1],
            device_id={"seq": seq_at((yi + o) % Y, xi, ci)}, device_id_type=MESH,
        )

    def b_last(o):
        return pltpu.make_async_remote_copy(
            src_ref=tb.at[o - 1], dst_ref=rb3.at[o - 1], send_sem=tbs.at[o - 1], recv_sem=tbr.at[o - 1],
            device_id={"seq": seq_at(yi, (xi + o) % X, ci)}, device_id_type=MESH,
        )

    def for_pair(turns):
        places = [ORDER[i] for i in turns]
        parts = [(j, h, p, o) for j, oy, ox in [(y * X + x, y, x) for y, x in places] for h, p, o in ((0, ox, oy), (1, oy, ox))]
        made = {oy * X + ox: grads(seq_at((yi + oy) % Y, (xi + ox) % X, ci)) for oy, ox in places}
        for j in made:
            pair_copy(j).wait_recv()
        for j, h, p, o in parts:
            if p % 2:
                far_copy(h, p // 2, o).wait_recv()
        for j, h, p, o in parts:
            ga, gb = made[j]
            for w in range(2):
                at = h * half + w * half // 2
                rows = slice(at, at + half // 2)
                va = ga[rows] + r1[j, rows, :depth].astype(F32)
                vb = gb[rows] + r1[j, rows, depth:].astype(F32)
                if p == 1 + 2 * w:
                    va = va + rf[h, w, o, :, :depth].astype(F32)
                    vb = vb + rf[h, w, o, :, depth:].astype(F32)
                to = slice(w * half // 2, (w + 1) * half // 2)
                sg[j, h, to, :depth] = va.astype(BF16)
                sg[j, h, to, depth:] = vb.astype(BF16)
        for j, h, p, o in parts:
            if p == 2:
                far_copy(h, 0, o).start()
                far_copy(h, 1, o).start()
            elif p:
                near_copy(h, p // 2, o).start()

    def column(o):
        for w in range(2):
            near_copy(0, w, o).wait_recv()
            near_copy(1, w, o).wait_recv()
        va, vb = (
            sg[slot_of(h, 0, o), h].astype(F32) + ra[h, 0, o].astype(F32) + ra[h, 1, o].astype(F32) for h in range(2)
        )
        if o == 0:
            fin[0], fin[1] = va, vb
        else:
            ta[o - 1], tb[o - 1] = va.astype(BF16), vb.astype(BF16)
            a_last(o).start()
            b_last(o).start()

    tab_copy.wait()
    for r in (2, 6, 1, 7):
        w_copy(r).wait()

    for i in range(8):
        for_sibling(range(2 * i, 2 * i + 2))
    for i in range(4):
        events((i, i), 2, False)
        for_pair(range(2 * i, 2 * i + 2))
    for i in range(4):
        events((i, i), 1, False)
        for_pair(range(8 + 2 * i, 10 + 2 * i))
        if i:
            column((0, 2, 1, 3)[i])

    def branch_block(b):
        v = jnp.dot(lall[b][:, :rank], uv[trial[b]], preferred_element_type=F32)
        branch[b] = ADAPTER_SCALE * v

    loop(blocks, branch_block, 8)

    def out_copy(q, i):
        target = seq_at((yi + q + 1) % Y, (xi + i // 2) % X, (ci + i) % C)
        return pltpu.make_async_remote_copy(
            src_ref=mix.at[target], dst_ref=out_h.at[si], send_sem=os.at[q, i], recv_sem=orr.at[q, i],
            device_id={"seq": target}, device_id_type=MESH,
        )

    def out_arrival(q, i):
        source = seq_at((yi + 2 * Y - q - 1) % Y, (xi + X - i // 2) % X, (ci + i) % C)
        return pltpu.make_async_remote_copy(
            src_ref=mix.at[source], dst_ref=out_h.at[source], send_sem=os.at[q, i], recv_sem=orr.at[q, i],
            device_id={"seq": source}, device_id_type=MESH,
        )

    self_copy = pltpu.make_async_copy(mix.at[si], out_h.at[si], loc.at[0])
    w_copy(0).wait()

    def finish(q):
        v = own(q, 0)
        for dr in range(2):
            z_copy(dr, q, 1).wait_recv()
        v = v + rbuf[0, q, 0].astype(F32) + rbuf[1, q, 0].astype(F32)
        at = pl.ds(rows_of(q), per)
        mix[at] = (v.reshape(per, blk, cols) + branch[at]).astype(BF16)

        def send(i):
            @pl.when(q * per + i != (CHUNKS - 1) * per)
            def _():
                out_copy(q, i).start()

        loop(per, send)

    finish(0)
    column(0)
    finish(1)
    finish(2)
    finish(3)
    self_copy.start()

    for o in range(1, 4):
        a_last(o).wait_recv()
        b_last(o).wait_recv()
    for h, last in ((0, ra3), (1, rb3)):
        v = fin[h]
        for p in range(3):
            v = v + last[p].astype(F32)
        v = ADAPTER_SCALE * v
        ga_v[h * half : (h + 1) * half] = v[:, :depth]
        gb_v[h * half : (h + 1) * half] = v[:, depth:]
    ga_copy = pltpu.make_async_copy(ga_v, ga_o.at[0], loc.at[1])
    gb_copy = pltpu.make_async_copy(gb_v, gb_o.at[0], loc.at[2])
    ga_copy.start()
    gb_copy.start()

    loop(4, lambda i: z_copy(i % 2, 2 * (i % 2) + i // 2, 4).wait_send())
    loop(24, lambda i: z_copy(i % 2, (i // 2) % 4, i // 8 + 1).wait_send())
    for o in range(1, Z):
        l_copy(o).wait_send()
        gather_copy(o, zi).wait_send()
    loop(X * Y, lambda j: pair_copy(j).wait_send())
    for o in range(4):
        for w in range(2):
            for h in range(2):
                far_copy(h, w, o).wait_send()
                near_copy(h, w, o).wait_send()
    for o in range(1, 4):
        a_last(o).wait_send()
        b_last(o).wait_send()

    def out_wait(n):
        @pl.when(n != (CHUNKS - 1) * per)
        def _():
            out_copy(n // per, n % per).wait_send()
            out_arrival(n // per, n % per).wait_recv()

    loop(blocks, out_wait)
    self_copy.wait()
    ga_copy.wait()
    gb_copy.wait()


def place(out, ga, gb, out_o, ga_o, gb_o, out_v, ga_v, gb_v, get, put):
    ways = ((out, out_v, out_o), (ga, ga_v, ga_o), (gb, gb_v, gb_o))
    gets = [pltpu.make_async_copy(a, v, get.at[i]) for i, (a, v, b) in enumerate(ways)]
    puts = [pltpu.make_async_copy(v, b, put.at[i]) for i, (a, v, b) in enumerate(ways)]
    for copy in gets:
        copy.start()
    for i in range(3):
        gets[i].wait()
        puts[i].start()
    for copy in puts:
        copy.wait()


def local(x, g, trial_per_block, trial_slot_index, w, down, up):
    blocks = trial_per_block.shape[0]
    trials, depth, rank = down.shape
    cols = up.shape[2]
    blk = x.shape[0] // blocks
    half, wide = rank // 2, depth + cols
    chunk = x.shape[0] // CHUNKS
    hbm = pl.BlockSpec(memory_space=pl.ANY)
    vmem = pl.BlockSpec(memory_space=pltpu.VMEM)
    dma = pltpu.SemaphoreType.DMA
    out, ga, gb = pl.pallas_call(
        kernel,
        out_shape=(
            jax.ShapeDtypeStruct((SEQ, blk, cols), BF16),
            jax.ShapeDtypeStruct((1, rank, depth), F32),
            jax.ShapeDtypeStruct((1, rank, cols), F32),
        ),
        in_specs=[pl.BlockSpec(memory_space=pltpu.SMEM)] * 2 + [vmem] + [hbm] * 5,
        out_specs=(hbm,) * 3,
        scratch_shapes=[
            pltpu.VMEM((trials, 128), jnp.int32),
            pltpu.SMEM((trials, 128), jnp.int32),
            pltpu.VMEM((blocks, blk, depth), BF16),
            pltpu.VMEM((blocks, blk, cols), BF16),
            pltpu.VMEM((Z, depth, cols), BF16),
            pltpu.VMEM((trials, rank, depth), BF16),
            pltpu.VMEM((trials, rank, cols), BF16),
            pltpu.VMEM((2, CHUNKS, 4, chunk, cols), BF16),
            pltpu.VMEM((2, CHUNKS, 4, chunk, cols), BF16),
            pltpu.VMEM((4, blk, 2 * rank), F32),
            pltpu.VMEM((blocks, blk, 2 * rank), RANK_SENT),
            pltpu.VMEM((Z - 1, 4, blk, 2 * rank), RANK_SENT),
            pltpu.VMEM((blocks, blk, 2 * rank), BF16),
            pltpu.VMEM((X * Y, rank, wide), BF16),
            pltpu.VMEM((X * Y, rank, wide), BF16),
            pltpu.VMEM((X * Y, 2, half, wide), BF16),
            pltpu.VMEM((2, 2, 4, half // 2, wide), BF16),
            pltpu.VMEM((2, 2, 4, half, wide), BF16),
            pltpu.VMEM((3, half, wide), BF16),
            pltpu.VMEM((3, half, wide), BF16),
            pltpu.VMEM((3, half, wide), BF16),
            pltpu.VMEM((3, half, wide), BF16),
            pltpu.VMEM((2, half, wide), F32),
            pltpu.VMEM((blocks, blk, cols), F32),
            pltpu.VMEM((blocks, blk, cols), BF16),
            pltpu.VMEM((rank, depth), F32),
            pltpu.VMEM((rank, cols), F32),
            dma((13,)),
            dma((2, CHUNKS, 4)), dma((2, CHUNKS, 4)),
            dma((Z - 1,)), dma((Z - 1,)),
            dma((Z - 1,)), dma((Z - 1,)),
            dma((X * Y,)), dma((X * Y,)),
            dma((2, 2, 4)), dma((2, 2, 4)), dma((2, 2, 4)), dma((2, 2, 4)),
            dma((3,)), dma((3,)), dma((3,)), dma((3,)),
            dma((CHUNKS, blocks // CHUNKS)), dma((CHUNKS, blocks // CHUNKS)),
            dma((3,)),
        ],
        compiler_params=pltpu.CompilerParams(collective_id=0, has_side_effects=True, vmem_limit_bytes=56 * 2**20),
    )(
        trial_per_block.reshape(blocks), trial_slot_index, trial_per_block.reshape(1, blocks),
        x.reshape(blocks, blk, depth), g.reshape(blocks, blk, cols), w, jnp.transpose(down, (0, 2, 1)), up,
    )
    out, ga, gb = pl.pallas_call(
        place,
        out_shape=tuple(jax.ShapeDtypeStruct(v.shape, v.dtype) for v in (out, ga, gb)),
        in_specs=[hbm] * 3,
        out_specs=(hbm,) * 3,
        scratch_shapes=[pltpu.VMEM(v.shape, v.dtype) for v in (out, ga, gb)] + [dma((3,)), dma((3,))],
    )(out, ga, gb)
    return out.reshape(x.shape[0], cols), jnp.transpose(ga, (0, 2, 1)), gb


def solution(mesh):
    in_specs = (
        P("seq", "grp"),
        P("seq", "grp"),
        P("seq", None),
        P(),
        P("grp", None),
        P(None, "grp", None),
        P(None, None, "grp"),
    )
    out_specs = (P("seq", "grp"), P("seq", "grp", None), P("seq", None, "grp"))
    return jax.shard_map(local, mesh=mesh, in_specs=in_specs, out_specs=out_specs, check_vma=False)
```

```python
import jax
import jax.numpy as jnp
from jax import lax
from jax.experimental import pallas as pl
from jax.experimental.pallas import tpu as pltpu
from jax.sharding import PartitionSpec as P

ADAPTER_SCALE = 2.0
MESH = pl.DeviceIdType.MESH
F32, BF16 = jnp.float32, jnp.bfloat16
RANK_SENT = BF16
NT = (((1,), (1,)), ((), ()))
TN = (((0,), (0,)), ((), ()))
Z, Y, X, C = 8, 4, 4, 2
SEQ = Y * X * C
CHUNKS = 4


ORDER = (
    (2, 2), (0, 2), (2, 0), (1, 2), (3, 2), (2, 1), (2, 3), (1, 1),
    (1, 3), (3, 1), (3, 3), (0, 1), (0, 3), (1, 0), (3, 0), (0, 0),
)


def loop(n, body, unroll=1):
    lax.fori_loop(0, n, lambda i, c: (body(i), c)[1], 0, unroll=unroll)


def kernel(
    trial, slot, trial_row, x_h, g_h, w_h, d_h, u_h, out_h, ga_o, gb_o,
    tab_v, tab, xv, gv, wv, dv, uv, sbuf, rbuf, lp, lsb, lrb, lall, s1, r1, sg, rf, ra, ta, tb, ra3, rb3, fin, branch, mix, ga_v, gb_v,
    ld_sem, zs, zr, ls, lr, ags, agr, s1s, s1r, rfs, rfr, ras, rar, tas, tar, tbs, tbr, os, orr, loc,
):
    zi, si = lax.axis_index("grp"), lax.axis_index("seq")
    ci, xi, yi = si % C, (si // C) % X, si // (C * X)
    blocks, blk, depth = xv.shape
    cols = gv.shape[2]
    rank = dv.shape[1]
    half = rank // 2
    per = blocks // CHUNKS
    wide = depth + cols

    def seq_at(y, x, c):
        return (y * X + x) * C + c

    barrier = pltpu.get_barrier_semaphore()
    loop(SEQ - 1, lambda o: pl.semaphore_signal(barrier, inc=1, device_id={"seq": (si + o + 1) % SEQ}, device_id_type=MESH))
    loop(Z - 1, lambda o: pl.semaphore_signal(barrier, inc=1, device_id={"grp": (zi + o + 1) % Z}, device_id_type=MESH))

    def w_copy(r):
        at = pl.multiple_of(((zi + r) % Z) * cols, cols)
        return pltpu.make_async_copy(w_h.at[:, pl.ds(at, cols)], wv.at[r], ld_sem.at[r])

    x_copy = pltpu.make_async_copy(x_h, xv, ld_sem.at[8])
    g_copy = pltpu.make_async_copy(g_h, gv, ld_sem.at[9])
    d_copy = pltpu.make_async_copy(d_h, dv, ld_sem.at[10])
    u_copy = pltpu.make_async_copy(u_h, uv, ld_sem.at[11])
    x_copy.start()
    w_copy(4).start()
    d_copy.start()
    g_copy.start()
    u_copy.start()
    for r in (3, 5, 2, 6, 1, 7, 0):
        w_copy(r).start()

    def rows_of(q):
        return ((yi + q + 1) % Y) * per

    def own(q, r):
        rows = xv[pl.ds(rows_of(q), per)].reshape(per * blk, depth)
        return jnp.dot(rows, wv[r], preferred_element_type=F32)

    def z_copy(dr, q, d):
        return pltpu.make_async_remote_copy(
            src_ref=sbuf.at[dr, q, d - 1], dst_ref=rbuf.at[dr, q, d - 1],
            send_sem=zs.at[dr, q, d - 1], recv_sem=zr.at[dr, q, d - 1],
            device_id={"grp": (zi + 1 - 2 * dr + Z) % Z}, device_id_type=MESH,
        )

    def events(places, d, first):
        sums = [own(q, ((1 - 2 * dr) * d + Z) % Z) for dr, q in enumerate(places)]
        if not first:
            for dr, q in enumerate(places):
                z_copy(dr, q, d + 1).wait_recv()
            sums = [v + rbuf[dr, q, d].astype(F32) for v, (dr, q) in zip(sums, enumerate(places))]
        for v, (dr, q) in zip(sums, enumerate(places)):
            sbuf[dr, q, d - 1] = v.astype(BF16)
        for dr, q in enumerate(places):
            z_copy(dr, q, d).start()

    def l_copy(o):
        return pltpu.make_async_remote_copy(
            src_ref=lsb.at[pl.ds(((zi + o) % Z) * 4, 4)], dst_ref=lrb.at[o - 1], send_sem=ls.at[o - 1], recv_sem=lr.at[o - 1],
            device_id={"grp": (zi + (1 if o == 4 else o)) % Z}, device_id_type=MESH,
        )

    def gather_copy(o, source):
        at = pl.ds(source * 4, 4)
        return pltpu.make_async_remote_copy(
            src_ref=lall.at[at], dst_ref=lall.at[at], send_sem=ags.at[o - 1], recv_sem=agr.at[o - 1],
            device_id={"grp": (zi + (7 if o == 4 else o)) % Z}, device_id_type=MESH,
        )

    count = slot.shape[0]
    slot_row = jnp.zeros((1, blocks), jnp.int32)
    for t in range(count):
        slot_row = jnp.where(trial_row[...] == t, slot[t], slot_row)
    here = jnp.broadcast_to(slot_row, (count, blocks)) == lax.broadcasted_iota(jnp.int32, (count, blocks), 0)
    number = lax.broadcasted_iota(jnp.int32, (count, blocks), 1)
    first = jnp.min(jnp.where(here, number, blocks), axis=1, keepdims=True)
    last = jnp.max(jnp.where(here, number, -1), axis=1, keepdims=True)
    lane = lax.broadcasted_iota(jnp.int32, tab_v.shape, 1)
    row = jnp.where(lane == 0, jnp.minimum(first, blocks - 1), jnp.maximum(last, 0))
    row = jnp.where(lane == 2, (last >= 0).astype(jnp.int32), row)
    tab_v[...] = jnp.where(lane == 3, (last > first).astype(jnp.int32), row)
    tab_copy = pltpu.make_async_copy(tab_v, tab, ld_sem.at[12])
    tab_copy.start()

    x_copy.wait()
    w_copy(4).wait()
    for q in range(CHUNKS):
        sbuf[q // 2, q, 3] = own(q, 4).astype(BF16)
    pl.semaphore_wait(barrier, SEQ - 1 + Z - 1)
    for q in (0, 2, 1, 3):
        z_copy(q // 2, q, 4).start()

    d_copy.wait()
    g_copy.wait()
    u_copy.wait()

    def rank_sums(o):
        made = []
        for n in range(4):
            b = ((zi + o) % Z) * 4 + n
            t = trial[b]
            down = lax.dot_general(xv[b], dv[t], NT, preferred_element_type=F32)
            back = lax.dot_general(gv[b], uv[t], NT, preferred_element_type=F32)
            made.append(jnp.concatenate([down, back], axis=1))
        return made

    for o in (4, 5, 2, 6, 1, 7):
        for n, v in enumerate(rank_sums(o)):
            lsb[((zi + o) % Z) * 4 + n] = v.astype(RANK_SENT)
        l_copy(o).start()
    for n, v in enumerate(rank_sums(0)):
        lp[n] = v
    made = rank_sums(3)
    l_copy(4).wait_recv()
    for n, v in enumerate(made):
        lsb[((zi + 3) % Z) * 4 + n] = (v + lrb[3, n].astype(F32)).astype(RANK_SENT)
    l_copy(3).start()
    for r in (3, 5):
        w_copy(r).wait()
    for i in range(2):
        events((2 + i, i), 3, True)
    mine = pl.ds(zi * 4, 4)
    v = lp[...]
    for o in (1, 2, 3, 5, 6, 7):
        l_copy(o).wait_recv()
        v = v + lrb[o - 1].astype(F32)
    lall[mine] = v.astype(BF16)
    for o in (5, 3, 2, 6, 1, 7):
        gather_copy(o, zi).start()
    for i in range(2):
        events((i, 2 + i), 3, False)

    gather_copy(5, (zi + 3) % Z).wait_recv()
    gather_copy(4, (zi + 3) % Z).start()
    for o in (1, 2, 3, 6, 7, 4):
        gather_copy(o, (zi - o + Z) % Z).wait_recv()

    def grads(k):
        b1, b2 = tab[k, 0], tab[k, 1]
        m1, m2 = tab[k, 2].astype(F32), tab[k, 3].astype(F32)
        rows = jnp.concatenate([lall[b1].astype(F32) * m1, lall[b2].astype(F32) * m2], axis=0).astype(BF16)
        xs = jnp.concatenate([xv[b1], xv[b2]], axis=0)
        gs = jnp.concatenate([gv[b1], gv[b2]], axis=0)
        return (
            lax.dot_general(rows[:, rank:], xs, TN, preferred_element_type=F32),
            lax.dot_general(rows[:, :rank], gs, TN, preferred_element_type=F32),
        )

    def pair_copy(j):
        return pltpu.make_async_remote_copy(
            src_ref=s1.at[j], dst_ref=r1.at[j], send_sem=s1s.at[j], recv_sem=s1r.at[j],
            device_id={"seq": seq_at(yi, xi, 1 - ci)}, device_id_type=MESH,
        )

    def for_sibling(turns):
        places = [ORDER[i] for i in turns]
        made = [grads(seq_at((yi + oy) % Y, (xi + ox) % X, 1 - ci)) for oy, ox in places]
        for (oy, ox), (ga, gb) in zip(places, made):
            s1[oy * X + ox, :, :depth] = ga.astype(BF16)
            s1[oy * X + ox, :, depth:] = gb.astype(BF16)
        for oy, ox in places:
            pair_copy(oy * X + ox).start()

    def slot_of(h, p, o):
        return o * X + p if h == 0 else p * X + o

    def along(h, p):
        return {"seq": seq_at(yi, (xi + p) % X, ci) if h == 0 else seq_at((yi + p) % Y, xi, ci)}

    def far_copy(h, w, o):
        return pltpu.make_async_remote_copy(
            src_ref=sg.at[slot_of(h, 2, o), h, pl.ds(w * half // 2, half // 2)], dst_ref=rf.at[h, w, o],
            send_sem=rfs.at[h, w, o], recv_sem=rfr.at[h, w, o], device_id=along(h, 1 + 2 * w), device_id_type=MESH,
        )

    def near_copy(h, w, o):
        return pltpu.make_async_remote_copy(
            src_ref=sg.at[slot_of(h, 1 + 2 * w, o), h], dst_ref=ra.at[h, w, o],
            send_sem=ras.at[h, w, o], recv_sem=rar.at[h, w, o], device_id=along(h, 1 + 2 * w), device_id_type=MESH,
        )

    def a_last(o):
        return pltpu.make_async_remote_copy(
            src_ref=ta.at[o - 1], dst_ref=ra3.at[o - 1], send_sem=tas.at[o - 1], recv_sem=tar.at[o - 1],
            device_id={"seq": seq_at((yi + o) % Y, xi, ci)}, device_id_type=MESH,
        )

    def b_last(o):
        return pltpu.make_async_remote_copy(
            src_ref=tb.at[o - 1], dst_ref=rb3.at[o - 1], send_sem=tbs.at[o - 1], recv_sem=tbr.at[o - 1],
            device_id={"seq": seq_at(yi, (xi + o) % X, ci)}, device_id_type=MESH,
        )

    def for_pair(turns):
        places = [ORDER[i] for i in turns]
        parts = [(j, h, p, o) for j, oy, ox in [(y * X + x, y, x) for y, x in places] for h, p, o in ((0, ox, oy), (1, oy, ox))]
        made = {oy * X + ox: grads(seq_at((yi + oy) % Y, (xi + ox) % X, ci)) for oy, ox in places}
        for j in made:
            pair_copy(j).wait_recv()
        for j, h, p, o in parts:
            if p % 2:
                far_copy(h, p // 2, o).wait_recv()
        for j, h, p, o in parts:
            ga, gb = made[j]
            for w in range(2):
                at = h * half + w * half // 2
                rows = slice(at, at + half // 2)
                va = ga[rows] + r1[j, rows, :depth].astype(F32)
                vb = gb[rows] + r1[j, rows, depth:].astype(F32)
                if p == 1 + 2 * w:
                    va = va + rf[h, w, o, :, :depth].astype(F32)
                    vb = vb + rf[h, w, o, :, depth:].astype(F32)
                to = slice(w * half // 2, (w + 1) * half // 2)
                sg[j, h, to, :depth] = va.astype(BF16)
                sg[j, h, to, depth:] = vb.astype(BF16)
        for j, h, p, o in parts:
            if p == 2:
                far_copy(h, 0, o).start()
                far_copy(h, 1, o).start()
            elif p:
                near_copy(h, p // 2, o).start()

    def column(o):
        for w in range(2):
            near_copy(0, w, o).wait_recv()
            near_copy(1, w, o).wait_recv()
        va, vb = (
            sg[slot_of(h, 0, o), h].astype(F32) + ra[h, 0, o].astype(F32) + ra[h, 1, o].astype(F32) for h in range(2)
        )
        if o == 0:
            fin[0], fin[1] = va, vb
        else:
            ta[o - 1], tb[o - 1] = va.astype(BF16), vb.astype(BF16)
            a_last(o).start()
            b_last(o).start()

    tab_copy.wait()
    for r in (2, 6, 1, 7):
        w_copy(r).wait()

    for i in range(8):
        for_sibling(range(2 * i, 2 * i + 2))
    for i in range(4):
        events((i, i), 2, False)
        for_pair(range(2 * i, 2 * i + 2))
    for i in range(4):
        events((i, i), 1, False)
        for_pair(range(8 + 2 * i, 10 + 2 * i))

    def branch_block(b):
        v = jnp.dot(lall[b][:, :rank], uv[trial[b]], preferred_element_type=F32)
        branch[b] = ADAPTER_SCALE * v

    loop(blocks, branch_block, 8)

    def out_copy(q, i):
        target = seq_at((yi + q + 1) % Y, (xi + i // 2) % X, (ci + i) % C)
        return pltpu.make_async_remote_copy(
            src_ref=mix.at[target], dst_ref=out_h.at[si], send_sem=os.at[q, i], recv_sem=orr.at[q, i],
            device_id={"seq": target}, device_id_type=MESH,
        )

    def out_arrival(q, i):
        source = seq_at((yi + 2 * Y - q - 1) % Y, (xi + X - i // 2) % X, (ci + i) % C)
        return pltpu.make_async_remote_copy(
            src_ref=mix.at[source], dst_ref=out_h.at[source], send_sem=os.at[q, i], recv_sem=orr.at[q, i],
            device_id={"seq": source}, device_id_type=MESH,
        )

    self_copy = pltpu.make_async_copy(mix.at[si], out_h.at[si], loc.at[0])
    w_copy(0).wait()

    def finish(q):
        v = own(q, 0)
        for dr in range(2):
            z_copy(dr, q, 1).wait_recv()
        v = v + rbuf[0, q, 0].astype(F32) + rbuf[1, q, 0].astype(F32)
        at = pl.ds(rows_of(q), per)
        mix[at] = (v.reshape(per, blk, cols) + branch[at]).astype(BF16)

        def send(i):
            @pl.when(q * per + i != (CHUNKS - 1) * per)
            def _():
                out_copy(q, i).start()

        loop(per, send)

    column(2)
    column(1)
    finish(0)
    column(3)
    column(0)
    finish(1)
    finish(2)
    finish(3)
    self_copy.start()

    for o in range(1, 4):
        a_last(o).wait_recv()
        b_last(o).wait_recv()
    for h, last in ((0, ra3), (1, rb3)):
        v = fin[h]
        for p in range(3):
            v = v + last[p].astype(F32)
        v = ADAPTER_SCALE * v
        ga_v[h * half : (h + 1) * half] = v[:, :depth]
        gb_v[h * half : (h + 1) * half] = v[:, depth:]
    ga_copy = pltpu.make_async_copy(ga_v, ga_o.at[0], loc.at[1])
    gb_copy = pltpu.make_async_copy(gb_v, gb_o.at[0], loc.at[2])
    ga_copy.start()
    gb_copy.start()

    loop(4, lambda i: z_copy(i % 2, 2 * (i % 2) + i // 2, 4).wait_send())
    loop(24, lambda i: z_copy(i % 2, (i // 2) % 4, i // 8 + 1).wait_send())
    for o in range(1, Z):
        l_copy(o).wait_send()
        gather_copy(o, (zi + 3) % Z if o == 4 else zi).wait_send()
    loop(X * Y, lambda j: pair_copy(j).wait_send())
    for o in range(4):
        for w in range(2):
            for h in range(2):
                far_copy(h, w, o).wait_send()
                near_copy(h, w, o).wait_send()
    for o in range(1, 4):
        a_last(o).wait_send()
        b_last(o).wait_send()

    def out_wait(n):
        @pl.when(n != (CHUNKS - 1) * per)
        def _():
            out_copy(n // per, n % per).wait_send()
            out_arrival(n // per, n % per).wait_recv()

    loop(blocks, out_wait)
    self_copy.wait()
    ga_copy.wait()
    gb_copy.wait()


def place(out, ga, gb, out_o, ga_o, gb_o, out_v, ga_v, gb_v, get, put):
    ways = ((out, out_v, out_o), (ga, ga_v, ga_o), (gb, gb_v, gb_o))
    gets = [pltpu.make_async_copy(a, v, get.at[i]) for i, (a, v, b) in enumerate(ways)]
    puts = [pltpu.make_async_copy(v, b, put.at[i]) for i, (a, v, b) in enumerate(ways)]
    for copy in gets:
        copy.start()
    for i in range(3):
        gets[i].wait()
        puts[i].start()
    for copy in puts:
        copy.wait()


def local(x, g, trial_per_block, trial_slot_index, w, down, up):
    blocks = trial_per_block.shape[0]
    trials, depth, rank = down.shape
    cols = up.shape[2]
    blk = x.shape[0] // blocks
    half, wide = rank // 2, depth + cols
    chunk = x.shape[0] // CHUNKS
    hbm = pl.BlockSpec(memory_space=pl.ANY)
    vmem = pl.BlockSpec(memory_space=pltpu.VMEM)
    dma = pltpu.SemaphoreType.DMA
    out, ga, gb = pl.pallas_call(
        kernel,
        out_shape=(
            jax.ShapeDtypeStruct((SEQ, blk, cols), BF16),
            jax.ShapeDtypeStruct((1, rank, depth), F32),
            jax.ShapeDtypeStruct((1, rank, cols), F32),
        ),
        in_specs=[pl.BlockSpec(memory_space=pltpu.SMEM)] * 2 + [vmem] + [hbm] * 5,
        out_specs=(hbm,) * 3,
        scratch_shapes=[
            pltpu.VMEM((trials, 128), jnp.int32),
            pltpu.SMEM((trials, 128), jnp.int32),
            pltpu.VMEM((blocks, blk, depth), BF16),
            pltpu.VMEM((blocks, blk, cols), BF16),
            pltpu.VMEM((Z, depth, cols), BF16),
            pltpu.VMEM((trials, rank, depth), BF16),
            pltpu.VMEM((trials, rank, cols), BF16),
            pltpu.VMEM((2, CHUNKS, 4, chunk, cols), BF16),
            pltpu.VMEM((2, CHUNKS, 4, chunk, cols), BF16),
            pltpu.VMEM((4, blk, 2 * rank), F32),
            pltpu.VMEM((blocks, blk, 2 * rank), RANK_SENT),
            pltpu.VMEM((Z - 1, 4, blk, 2 * rank), RANK_SENT),
            pltpu.VMEM((blocks, blk, 2 * rank), BF16),
            pltpu.VMEM((X * Y, rank, wide), BF16),
            pltpu.VMEM((X * Y, rank, wide), BF16),
            pltpu.VMEM((X * Y, 2, half, wide), BF16),
            pltpu.VMEM((2, 2, 4, half // 2, wide), BF16),
            pltpu.VMEM((2, 2, 4, half, wide), BF16),
            pltpu.VMEM((3, half, wide), BF16),
            pltpu.VMEM((3, half, wide), BF16),
            pltpu.VMEM((3, half, wide), BF16),
            pltpu.VMEM((3, half, wide), BF16),
            pltpu.VMEM((2, half, wide), F32),
            pltpu.VMEM((blocks, blk, cols), F32),
            pltpu.VMEM((blocks, blk, cols), BF16),
            pltpu.VMEM((rank, depth), F32),
            pltpu.VMEM((rank, cols), F32),
            dma((13,)),
            dma((2, CHUNKS, 4)), dma((2, CHUNKS, 4)),
            dma((Z - 1,)), dma((Z - 1,)),
            dma((Z - 1,)), dma((Z - 1,)),
            dma((X * Y,)), dma((X * Y,)),
            dma((2, 2, 4)), dma((2, 2, 4)), dma((2, 2, 4)), dma((2, 2, 4)),
            dma((3,)), dma((3,)), dma((3,)), dma((3,)),
            dma((CHUNKS, blocks // CHUNKS)), dma((CHUNKS, blocks // CHUNKS)),
            dma((3,)),
        ],
        compiler_params=pltpu.CompilerParams(collective_id=0, has_side_effects=True, vmem_limit_bytes=56 * 2**20),
    )(
        trial_per_block.reshape(blocks), trial_slot_index, trial_per_block.reshape(1, blocks),
        x.reshape(blocks, blk, depth), g.reshape(blocks, blk, cols), w, jnp.transpose(down, (0, 2, 1)), up,
    )
    out, ga, gb = pl.pallas_call(
        place,
        out_shape=tuple(jax.ShapeDtypeStruct(v.shape, v.dtype) for v in (out, ga, gb)),
        in_specs=[hbm] * 3,
        out_specs=(hbm,) * 3,
        scratch_shapes=[pltpu.VMEM(v.shape, v.dtype) for v in (out, ga, gb)] + [dma((3,)), dma((3,))],
    )(out, ga, gb)
    return out.reshape(x.shape[0], cols), jnp.transpose(ga, (0, 2, 1)), gb


def solution(mesh):
    in_specs = (
        P("seq", "grp"),
        P("seq", "grp"),
        P("seq", None),
        P(),
        P("grp", None),
        P(None, "grp", None),
        P(None, None, "grp"),
    )
    out_specs = (P("seq", "grp"), P("seq", "grp", None), P("seq", None, "grp"))
    return jax.shard_map(local, mesh=mesh, in_specs=in_specs, out_specs=out_specs, check_vma=False)
```

```python
import jax
import jax.numpy as jnp
from jax import lax
from jax.experimental import pallas as pl
from jax.experimental.pallas import tpu as pltpu
from jax.sharding import PartitionSpec as P

ADAPTER_SCALE = 2.0
MESH = pl.DeviceIdType.MESH
F32, BF16 = jnp.float32, jnp.bfloat16
RANK_SENT = BF16
NT = (((1,), (1,)), ((), ()))
TN = (((0,), (0,)), ((), ()))
Z, Y, X, C = 8, 4, 4, 2
SEQ = Y * X * C
CHUNKS = 4


ORDER = (
    (2, 2), (0, 2), (2, 0), (1, 2), (3, 2), (2, 1), (2, 3), (1, 1),
    (1, 3), (3, 1), (3, 3), (0, 1), (0, 3), (1, 0), (3, 0), (0, 0),
)


def loop(n, body, unroll=1):
    lax.fori_loop(0, n, lambda i, c: (body(i), c)[1], 0, unroll=unroll)


def kernel(
    trial, slot, trial_row, x_h, g_h, w_h, d_h, u_h, out_h, ga_o, gb_o,
    tab_v, tab, xv, gv, wv, dv, uv, sbuf, rbuf, lp, lsb, lrb, lall, s1, r1, sg, rf, ra, ta, tb, ra3, rb3, fin, branch, mix, ga_v, gb_v,
    ld_sem, zs, zr, ls, lr, ags, agr, s1s, s1r, rfs, rfr, ras, rar, tas, tar, tbs, tbr, os, orr, loc,
):
    zi, si = lax.axis_index("grp"), lax.axis_index("seq")
    ci, xi, yi = si % C, (si // C) % X, si // (C * X)
    blocks, blk, depth = xv.shape
    cols = gv.shape[2]
    rank = dv.shape[1]
    half = rank // 2
    per = blocks // CHUNKS
    wide = depth + cols

    def seq_at(y, x, c):
        return (y * X + x) * C + c

    barrier = pltpu.get_barrier_semaphore()
    loop(SEQ - 1, lambda o: pl.semaphore_signal(barrier, inc=1, device_id={"seq": (si + o + 1) % SEQ}, device_id_type=MESH))
    loop(Z - 1, lambda o: pl.semaphore_signal(barrier, inc=1, device_id={"grp": (zi + o + 1) % Z}, device_id_type=MESH))

    def w_copy(r):
        at = pl.multiple_of(((zi + r) % Z) * cols, cols)
        return pltpu.make_async_copy(w_h.at[:, pl.ds(at, cols)], wv.at[r], ld_sem.at[r])

    x_copy = pltpu.make_async_copy(x_h, xv, ld_sem.at[8])
    g_copy = pltpu.make_async_copy(g_h, gv, ld_sem.at[9])
    d_copy = pltpu.make_async_copy(d_h, dv, ld_sem.at[10])
    u_copy = pltpu.make_async_copy(u_h, uv, ld_sem.at[11])
    x_copy.start()
    w_copy(4).start()
    d_copy.start()
    g_copy.start()
    u_copy.start()
    for r in (3, 5, 2, 6, 1, 7, 0):
        w_copy(r).start()

    def rows_of(q):
        return ((yi + q + 1) % Y) * per

    def own(q, r):
        rows = xv[pl.ds(rows_of(q), per)].reshape(per * blk, depth)
        return jnp.dot(rows, wv[r], preferred_element_type=F32)

    def z_copy(dr, q, d):
        return pltpu.make_async_remote_copy(
            src_ref=sbuf.at[dr, q, d - 1], dst_ref=rbuf.at[dr, q, d - 1],
            send_sem=zs.at[dr, q, d - 1], recv_sem=zr.at[dr, q, d - 1],
            device_id={"grp": (zi + 1 - 2 * dr + Z) % Z}, device_id_type=MESH,
        )

    def events(places, d, first):
        sums = [own(q, ((1 - 2 * dr) * d + Z) % Z) for dr, q in enumerate(places)]
        if not first:
            for dr, q in enumerate(places):
                z_copy(dr, q, d + 1).wait_recv()
            sums = [v + rbuf[dr, q, d].astype(F32) for v, (dr, q) in zip(sums, enumerate(places))]
        for v, (dr, q) in zip(sums, enumerate(places)):
            sbuf[dr, q, d - 1] = v.astype(BF16)
        for dr, q in enumerate(places):
            z_copy(dr, q, d).start()

    def l_copy(o):
        return pltpu.make_async_remote_copy(
            src_ref=lsb.at[pl.ds(((zi + o) % Z) * 4, 4)], dst_ref=lrb.at[o - 1], send_sem=ls.at[o - 1], recv_sem=lr.at[o - 1],
            device_id={"grp": (zi + o) % Z}, device_id_type=MESH,
        )

    def gather_copy(o, source):
        at = pl.ds(source * 4, 4)
        return pltpu.make_async_remote_copy(
            src_ref=lall.at[at], dst_ref=lall.at[at], send_sem=ags.at[o - 1], recv_sem=agr.at[o - 1],
            device_id={"grp": (zi + o) % Z}, device_id_type=MESH,
        )

    count = slot.shape[0]
    slot_row = jnp.zeros((1, blocks), jnp.int32)
    for t in range(count):
        slot_row = jnp.where(trial_row[...] == t, slot[t], slot_row)
    here = jnp.broadcast_to(slot_row, (count, blocks)) == lax.broadcasted_iota(jnp.int32, (count, blocks), 0)
    number = lax.broadcasted_iota(jnp.int32, (count, blocks), 1)
    first = jnp.min(jnp.where(here, number, blocks), axis=1, keepdims=True)
    last = jnp.max(jnp.where(here, number, -1), axis=1, keepdims=True)
    lane = lax.broadcasted_iota(jnp.int32, tab_v.shape, 1)
    row = jnp.where(lane == 0, jnp.minimum(first, blocks - 1), jnp.maximum(last, 0))
    row = jnp.where(lane == 2, (last >= 0).astype(jnp.int32), row)
    tab_v[...] = jnp.where(lane == 3, (last > first).astype(jnp.int32), row)
    tab_copy = pltpu.make_async_copy(tab_v, tab, ld_sem.at[12])
    tab_copy.start()

    x_copy.wait()
    w_copy(4).wait()
    for q in range(CHUNKS):
        sbuf[q // 2, q, 3] = own(q, 4).astype(BF16)
    pl.semaphore_wait(barrier, SEQ - 1 + Z - 1)
    for q in (0, 2, 1, 3):
        z_copy(q // 2, q, 4).start()

    d_copy.wait()
    g_copy.wait()
    u_copy.wait()

    def rank_sums(o):
        made = []
        for n in range(4):
            b = ((zi + o) % Z) * 4 + n
            t = trial[b]
            down = lax.dot_general(xv[b], dv[t], NT, preferred_element_type=F32)
            back = lax.dot_general(gv[b], uv[t], NT, preferred_element_type=F32)
            made.append(jnp.concatenate([down, back], axis=1))
        return made

    for o in (4, 3, 5, 2, 6, 1, 7):
        for n, v in enumerate(rank_sums(o)):
            lsb[((zi + o) % Z) * 4 + n] = v.astype(RANK_SENT)
        l_copy(o).start()
    for n, v in enumerate(rank_sums(0)):
        lp[n] = v
    for r in (3, 5):
        w_copy(r).wait()
    events((2, 0), 3, True)
    mine = pl.ds(zi * 4, 4)
    v = lp[...]
    for o in range(1, Z):
        l_copy(o).wait_recv()
        v = v + lrb[o - 1].astype(F32)
    lall[mine] = v.astype(BF16)
    for o in (4, 3, 5, 2, 6, 1, 7):
        gather_copy(o, zi).start()
    events((3, 1), 3, True)
    for i in range(2):
        events((i, 2 + i), 3, False)

    for o in range(1, Z):
        gather_copy(o, (zi - o + Z) % Z).wait_recv()

    def grads(k):
        b1, b2 = tab[k, 0], tab[k, 1]
        m1, m2 = tab[k, 2].astype(F32), tab[k, 3].astype(F32)
        rows = jnp.concatenate([lall[b1].astype(F32) * m1, lall[b2].astype(F32) * m2], axis=0).astype(BF16)
        xs = jnp.concatenate([xv[b1], xv[b2]], axis=0)
        gs = jnp.concatenate([gv[b1], gv[b2]], axis=0)
        return (
            lax.dot_general(rows[:, rank:], xs, TN, preferred_element_type=F32),
            lax.dot_general(rows[:, :rank], gs, TN, preferred_element_type=F32),
        )

    def pair_copy(j):
        return pltpu.make_async_remote_copy(
            src_ref=s1.at[j], dst_ref=r1.at[j], send_sem=s1s.at[j], recv_sem=s1r.at[j],
            device_id={"seq": seq_at(yi, xi, 1 - ci)}, device_id_type=MESH,
        )

    def for_sibling(turns):
        places = [ORDER[i] for i in turns]
        made = [grads(seq_at((yi + oy) % Y, (xi + ox) % X, 1 - ci)) for oy, ox in places]
        for (oy, ox), (ga, gb) in zip(places, made):
            s1[oy * X + ox, :, :depth] = ga.astype(BF16)
            s1[oy * X + ox, :, depth:] = gb.astype(BF16)
        for oy, ox in places:
            pair_copy(oy * X + ox).start()

    def slot_of(h, p, o):
        return o * X + p if h == 0 else p * X + o

    def along(h, p):
        return {"seq": seq_at(yi, (xi + p) % X, ci) if h == 0 else seq_at((yi + p) % Y, xi, ci)}

    def far_copy(h, w, o):
        return pltpu.make_async_remote_copy(
            src_ref=sg.at[slot_of(h, 2, o), h, pl.ds(w * half // 2, half // 2)], dst_ref=rf.at[h, w, o],
            send_sem=rfs.at[h, w, o], recv_sem=rfr.at[h, w, o], device_id=along(h, 1 + 2 * w), device_id_type=MESH,
        )

    def near_copy(h, w, o):
        return pltpu.make_async_remote_copy(
            src_ref=sg.at[slot_of(h, 1 + 2 * w, o), h], dst_ref=ra.at[h, w, o],
            send_sem=ras.at[h, w, o], recv_sem=rar.at[h, w, o], device_id=along(h, 1 + 2 * w), device_id_type=MESH,
        )

    def a_last(o):
        return pltpu.make_async_remote_copy(
            src_ref=ta.at[o - 1], dst_ref=ra3.at[o - 1], send_sem=tas.at[o - 1], recv_sem=tar.at[o - 1],
            device_id={"seq": seq_at((yi + o) % Y, xi, ci)}, device_id_type=MESH,
        )

    def b_last(o):
        return pltpu.make_async_remote_copy(
            src_ref=tb.at[o - 1], dst_ref=rb3.at[o - 1], send_sem=tbs.at[o - 1], recv_sem=tbr.at[o - 1],
            device_id={"seq": seq_at(yi, (xi + o) % X, ci)}, device_id_type=MESH,
        )

    def for_pair(turns):
        places = [ORDER[i] for i in turns]
        parts = [(j, h, p, o) for j, oy, ox in [(y * X + x, y, x) for y, x in places] for h, p, o in ((0, ox, oy), (1, oy, ox))]
        made = {oy * X + ox: grads(seq_at((yi + oy) % Y, (xi + ox) % X, ci)) for oy, ox in places}
        for j in made:
            pair_copy(j).wait_recv()
        for j, h, p, o in parts:
            if p % 2:
                far_copy(h, p // 2, o).wait_recv()
        for j, h, p, o in parts:
            ga, gb = made[j]
            for w in range(2):
                at = h * half + w * half // 2
                rows = slice(at, at + half // 2)
                va = ga[rows] + r1[j, rows, :depth].astype(F32)
                vb = gb[rows] + r1[j, rows, depth:].astype(F32)
                if p == 1 + 2 * w:
                    va = va + rf[h, w, o, :, :depth].astype(F32)
                    vb = vb + rf[h, w, o, :, depth:].astype(F32)
                to = slice(w * half // 2, (w + 1) * half // 2)
                sg[j, h, to, :depth] = va.astype(BF16)
                sg[j, h, to, depth:] = vb.astype(BF16)
        for j, h, p, o in parts:
            if p == 2:
                far_copy(h, 0, o).start()
                far_copy(h, 1, o).start()
            elif p:
                near_copy(h, p // 2, o).start()

    def column(o):
        for w in range(2):
            near_copy(0, w, o).wait_recv()
            near_copy(1, w, o).wait_recv()
        va, vb = (
            sg[slot_of(h, 0, o), h].astype(F32) + ra[h, 0, o].astype(F32) + ra[h, 1, o].astype(F32) for h in range(2)
        )
        if o == 0:
            fin[0], fin[1] = va, vb
        else:
            ta[o - 1], tb[o - 1] = va.astype(BF16), vb.astype(BF16)
            a_last(o).start()
            b_last(o).start()

    tab_copy.wait()
    for r in (2, 6, 1, 7):
        w_copy(r).wait()

    for i in range(8):
        for_sibling(range(2 * i, 2 * i + 2))
    for i in range(4):
        events((i, i), 2, False)
        for_pair(range(2 * i, 2 * i + 2))
    for i in range(4):
        events((i, i), 1, False)
        for_pair(range(8 + 2 * i, 10 + 2 * i))

    def branch_block(b):
        v = jnp.dot(lall[b][:, :rank], uv[trial[b]], preferred_element_type=F32)
        branch[b] = ADAPTER_SCALE * v

    loop(blocks, branch_block, 8)

    def out_copy(q, i):
        target = seq_at((yi + q + 1) % Y, (xi + i // 2) % X, (ci + i) % C)
        return pltpu.make_async_remote_copy(
            src_ref=mix.at[target], dst_ref=out_h.at[si], send_sem=os.at[q, i], recv_sem=orr.at[q, i],
            device_id={"seq": target}, device_id_type=MESH,
        )

    def out_arrival(q, i):
        source = seq_at((yi + 2 * Y - q - 1) % Y, (xi + X - i // 2) % X, (ci + i) % C)
        return pltpu.make_async_remote_copy(
            src_ref=mix.at[source], dst_ref=out_h.at[source], send_sem=os.at[q, i], recv_sem=orr.at[q, i],
            device_id={"seq": source}, device_id_type=MESH,
        )

    self_copy = pltpu.make_async_copy(mix.at[si], out_h.at[si], loc.at[0])
    w_copy(0).wait()

    def finish(q):
        v = own(q, 0)
        for dr in range(2):
            z_copy(dr, q, 1).wait_recv()
        v = v + rbuf[0, q, 0].astype(F32) + rbuf[1, q, 0].astype(F32)
        at = pl.ds(rows_of(q), per)
        mix[at] = (v.reshape(per, blk, cols) + branch[at]).astype(BF16)

        def send(i):
            @pl.when(q * per + i != (CHUNKS - 1) * per)
            def _():
                out_copy(q, i).start()

        loop(per, send)

    column(2)
    column(1)
    finish(0)
    column(3)
    column(0)
    finish(1)
    finish(2)
    finish(3)
    self_copy.start()

    for o in range(1, 4):
        a_last(o).wait_recv()
        b_last(o).wait_recv()
    for h, last in ((0, ra3), (1, rb3)):
        v = fin[h]
        for p in range(3):
            v = v + last[p].astype(F32)
        v = ADAPTER_SCALE * v
        ga_v[h * half : (h + 1) * half] = v[:, :depth]
        gb_v[h * half : (h + 1) * half] = v[:, depth:]
    ga_copy = pltpu.make_async_copy(ga_v, ga_o.at[0], loc.at[1])
    gb_copy = pltpu.make_async_copy(gb_v, gb_o.at[0], loc.at[2])
    ga_copy.start()
    gb_copy.start()

    loop(4, lambda i: z_copy(i % 2, 2 * (i % 2) + i // 2, 4).wait_send())
    loop(24, lambda i: z_copy(i % 2, (i // 2) % 4, i // 8 + 1).wait_send())
    for o in range(1, Z):
        l_copy(o).wait_send()
        gather_copy(o, zi).wait_send()
    loop(X * Y, lambda j: pair_copy(j).wait_send())
    for o in range(4):
        for w in range(2):
            for h in range(2):
                far_copy(h, w, o).wait_send()
                near_copy(h, w, o).wait_send()
    for o in range(1, 4):
        a_last(o).wait_send()
        b_last(o).wait_send()

    def out_wait(n):
        @pl.when(n != (CHUNKS - 1) * per)
        def _():
            out_copy(n // per, n % per).wait_send()
            out_arrival(n // per, n % per).wait_recv()

    loop(blocks, out_wait)
    self_copy.wait()
    ga_copy.wait()
    gb_copy.wait()


def place(out, ga, gb, out_o, ga_o, gb_o, out_v, ga_v, gb_v, get, put):
    ways = ((out, out_v, out_o), (ga, ga_v, ga_o), (gb, gb_v, gb_o))
    gets = [pltpu.make_async_copy(a, v, get.at[i]) for i, (a, v, b) in enumerate(ways)]
    puts = [pltpu.make_async_copy(v, b, put.at[i]) for i, (a, v, b) in enumerate(ways)]
    for copy in gets:
        copy.start()
    for i in range(3):
        gets[i].wait()
        puts[i].start()
    for copy in puts:
        copy.wait()


def local(x, g, trial_per_block, trial_slot_index, w, down, up):
    blocks = trial_per_block.shape[0]
    trials, depth, rank = down.shape
    cols = up.shape[2]
    blk = x.shape[0] // blocks
    half, wide = rank // 2, depth + cols
    chunk = x.shape[0] // CHUNKS
    hbm = pl.BlockSpec(memory_space=pl.ANY)
    vmem = pl.BlockSpec(memory_space=pltpu.VMEM)
    dma = pltpu.SemaphoreType.DMA
    out, ga, gb = pl.pallas_call(
        kernel,
        out_shape=(
            jax.ShapeDtypeStruct((SEQ, blk, cols), BF16),
            jax.ShapeDtypeStruct((1, rank, depth), F32),
            jax.ShapeDtypeStruct((1, rank, cols), F32),
        ),
        in_specs=[pl.BlockSpec(memory_space=pltpu.SMEM)] * 2 + [vmem] + [hbm] * 5,
        out_specs=(hbm,) * 3,
        scratch_shapes=[
            pltpu.VMEM((trials, 128), jnp.int32),
            pltpu.SMEM((trials, 128), jnp.int32),
            pltpu.VMEM((blocks, blk, depth), BF16),
            pltpu.VMEM((blocks, blk, cols), BF16),
            pltpu.VMEM((Z, depth, cols), BF16),
            pltpu.VMEM((trials, rank, depth), BF16),
            pltpu.VMEM((trials, rank, cols), BF16),
            pltpu.VMEM((2, CHUNKS, 4, chunk, cols), BF16),
            pltpu.VMEM((2, CHUNKS, 4, chunk, cols), BF16),
            pltpu.VMEM((4, blk, 2 * rank), F32),
            pltpu.VMEM((blocks, blk, 2 * rank), RANK_SENT),
            pltpu.VMEM((Z - 1, 4, blk, 2 * rank), RANK_SENT),
            pltpu.VMEM((blocks, blk, 2 * rank), BF16),
            pltpu.VMEM((X * Y, rank, wide), BF16),
            pltpu.VMEM((X * Y, rank, wide), BF16),
            pltpu.VMEM((X * Y, 2, half, wide), BF16),
            pltpu.VMEM((2, 2, 4, half // 2, wide), BF16),
            pltpu.VMEM((2, 2, 4, half, wide), BF16),
            pltpu.VMEM((3, half, wide), BF16),
            pltpu.VMEM((3, half, wide), BF16),
            pltpu.VMEM((3, half, wide), BF16),
            pltpu.VMEM((3, half, wide), BF16),
            pltpu.VMEM((2, half, wide), F32),
            pltpu.VMEM((blocks, blk, cols), F32),
            pltpu.VMEM((blocks, blk, cols), BF16),
            pltpu.VMEM((rank, depth), F32),
            pltpu.VMEM((rank, cols), F32),
            dma((13,)),
            dma((2, CHUNKS, 4)), dma((2, CHUNKS, 4)),
            dma((Z - 1,)), dma((Z - 1,)),
            dma((Z - 1,)), dma((Z - 1,)),
            dma((X * Y,)), dma((X * Y,)),
            dma((2, 2, 4)), dma((2, 2, 4)), dma((2, 2, 4)), dma((2, 2, 4)),
            dma((3,)), dma((3,)), dma((3,)), dma((3,)),
            dma((CHUNKS, blocks // CHUNKS)), dma((CHUNKS, blocks // CHUNKS)),
            dma((3,)),
        ],
        compiler_params=pltpu.CompilerParams(collective_id=0, has_side_effects=True, vmem_limit_bytes=56 * 2**20),
    )(
        trial_per_block.reshape(blocks), trial_slot_index, trial_per_block.reshape(1, blocks),
        x.reshape(blocks, blk, depth), g.reshape(blocks, blk, cols), w, jnp.transpose(down, (0, 2, 1)), up,
    )
    out, ga, gb = pl.pallas_call(
        place,
        out_shape=tuple(jax.ShapeDtypeStruct(v.shape, v.dtype) for v in (out, ga, gb)),
        in_specs=[hbm] * 3,
        out_specs=(hbm,) * 3,
        scratch_shapes=[pltpu.VMEM(v.shape, v.dtype) for v in (out, ga, gb)] + [dma((3,)), dma((3,))],
    )(out, ga, gb)
    return out.reshape(x.shape[0], cols), jnp.transpose(ga, (0, 2, 1)), gb


def solution(mesh):
    in_specs = (
        P("seq", "grp"),
        P("seq", "grp"),
        P("seq", None),
        P(),
        P("grp", None),
        P(None, "grp", None),
        P(None, None, "grp"),
    )
    out_specs = (P("seq", "grp"), P("seq", "grp", None), P("seq", None, "grp"))
    return jax.shard_map(local, mesh=mesh, in_specs=in_specs, out_specs=out_specs, check_vma=False)
```
